256 devices in a mesh: tower: 2 (over x_lo), dp: 32 (over x_hi, z, core), mp: 4 (over y).
Axes of the slice: x: 4 (x_hi: 2, x_lo: 2; x = x_hi * 2 + x_lo), y: 4, z: 8, core: 2. Of those that a mesh axis runs over, the one named last changes fastest.
Arguments:
- inputs: bfloat16 [2, 16384, 1792], P('tower', 'dp', 'mp'), may hold values from -6 to 6
- weights: bfloat16 [2, 1792, 1152], P('tower', 'mp'), may hold values from -0.125 to 0.125
- pair_ids: int32 [16384], P('dp'), may hold values from 0 to 32767
Outputs:
- row_loss: float32 [2, 16384], P('tower', 'dp')
- input_grad: bfloat16 [2, 16384, 1792], P('tower', 'dp', 'mp')
- weight_grad: float32 [2, 1792, 1152], P('tower', ('mp', 'dp'))
The draws below stay inside these ranges and needn't reach their ends.
Inputs may be any that keep to these rules, and one draw needn't show every extreme that they name: `pair_ids`: row i's image and text form pair i; rows with equal ids are positive pairs, all others negative.
All inputs are finite; a program needn't handle non-finite values.
Results may differ from the reference program's by a relative error of at most 0.015.
Values may be sent and summed in bfloat16 or wider, within the bound.
A program may use at most 64 MiB of HBM per device.

```python
import math
import jax
import jax.numpy as jnp
import numpy as np
from jax import lax

DI = 1792
E = 1152
B_DEV = 512
BATCH = 16384
N_DP = 32


def plant(entries, own_key, low, high):
    extent = entries.shape
    index_at = [jax.random.randint(jax.random.fold_in(own_key, axis), (), 0, extent[axis]) for axis in range(len(extent))]
    entries = entries.at[tuple(index_at)].set(low)
    longest = extent.index(max(extent))
    index_at[longest] = (index_at[longest] + 1) % extent[longest]
    return entries.at[tuple(index_at)].set(high)


def block_levels(rng, dims, split, least, high):
    loudness, own = 1.0, jax.random.fold_in(rng, 6)
    for position, parts in split:
        steps = jnp.exp(jax.random.uniform(jax.random.fold_in(own, position), (parts,), jnp.float32, least / len(split), high / len(split)))
        loudness = loudness * jnp.repeat(steps, dims[position] // parts).reshape([-1 if axis == position else 1 for axis in range(len(dims))])
    return loudness


def rank_table(amount, slope):
    portions = [(1 << 20) // math.isqrt(rank ** slope) + 1 for rank in range(1, amount + 1)]
    deviation = 1 + sum(portions) // (1 << 30)
    return np.cumsum(np.array([max(1, weight // deviation) for weight in portions]))


def ranked_ids(own_key, shape, count, lean):
    grid = rank_table(count, lean)
    lot = jax.random.randint(jax.random.fold_in(own_key, 1), shape, 0, int(grid[count - 1]))
    rank = jnp.searchsorted(jnp.asarray(grid, jnp.int32), lot, side="right")
    return jax.random.permutation(jax.random.fold_in(own_key, 2), count)[rank].astype(jnp.int32)


def noise(own_key, shape, spread, reach, pieces=(), kind=jnp.bfloat16):
    drawn = spread * jax.random.normal(own_key, shape, jnp.float32)
    if pieces:
        drawn = drawn * block_levels(own_key, shape, pieces, -0.22, 0.18)
    return jnp.clip(drawn, -reach, reach).astype(kind)


def setup_inputs(seed: int = 0) -> dict:
    splits = jax.random.split(jax.random.key(seed), 4)
    return {
        "inputs": noise(splits[0], (2, BATCH, DI), 1.0, 6.0, ((0, 2), (1, 32), (2, 4))),
        "weights": noise(splits[1], (2, DI, E), DI ** -0.5, 0.125, ((0, 2), (1, 4))),
        "pair_ids": plant(ranked_ids(splits[2], (BATCH,), 2 * BATCH, 1), jax.random.fold_in(splits[2], 3), 0, (2 * BATCH) - 1).astype(jnp.int32),
    }


logit_scale = 100.0
pair_logit_bias = -6.0
norm_eps = 1e-06

def pair_terms(local_unit_rows, own_ids, partner_unit_rows, other_ids):
    pair_logits = logit_scale * jnp.dot(local_unit_rows, partner_unit_rows.T, preferred_element_type=jnp.float32) + pair_logit_bias
    label_sign = jnp.where(own_ids[:, None] == other_ids[None, :], 1.0, -1.0).astype(jnp.float32)
    pair_loss = jax.nn.softplus(-label_sign * pair_logits)
    slope_bias_gradient = (-label_sign * jax.nn.sigmoid(-label_sign * pair_logits)).astype(jnp.bfloat16)
    return (pair_loss, slope_bias_gradient)

def tower_unit(features, weight):
    embedding = jnp.dot(features, weight, preferred_element_type=jnp.float32)
    inverse_norm = lax.rsqrt(lax.optimization_barrier(jnp.sum(embedding * embedding, axis=1, keepdims=True)) + norm_eps)
    return (embedding * inverse_norm, inverse_norm)

def tower_back(features, weight, unit_vec, inverse_norm, unit_grad):
    inner = lax.optimization_barrier(jnp.sum(unit_vec * unit_grad, axis=1, keepdims=True))
    delta_b = ((unit_grad - unit_vec * inner) * inverse_norm).astype(jnp.bfloat16)
    feature_grad = jnp.dot(delta_b, weight.T, preferred_element_type=jnp.float32).astype(jnp.bfloat16)
    matrix_grad = jnp.dot(features.T, delta_b, preferred_element_type=jnp.float32)
    return (feature_grad, matrix_grad)

def reference(inputs, weights, pair_ids):
    image_unit, image_norm = tower_unit(inputs[0], weights[0])
    text_unit, text_norm = tower_unit(inputs[1], weights[1])
    image_b = image_unit.astype(jnp.bfloat16)
    text_batch = text_unit.astype(jnp.bfloat16)

    def visit(totals, block_index):
        text_gradient, text_loss = totals
        row_start = (block_index * B_DEV).astype(jnp.int32)
        image_rows_block = lax.dynamic_slice_in_dim(image_b, row_start, B_DEV, 0)
        block_ids = lax.dynamic_slice_in_dim(pair_ids, row_start, B_DEV, 0)
        pair_loss, slope_bias_gradient = pair_terms(image_rows_block, block_ids, text_batch, pair_ids)
        image_gradient = logit_scale * jnp.dot(slope_bias_gradient, text_batch, preferred_element_type=jnp.float32)
        text_gradient = text_gradient + logit_scale * jnp.dot(slope_bias_gradient.T, image_rows_block, preferred_element_type=jnp.float32)
        text_loss = text_loss + lax.optimization_barrier(jnp.sum(pair_loss, axis=0))
        return ((text_gradient, text_loss), (image_gradient, lax.optimization_barrier(jnp.sum(pair_loss, axis=1))))
    start_totals = (jnp.zeros((BATCH, E), jnp.float32), jnp.zeros((BATCH,), jnp.float32))
    totals, per_block = lax.scan(visit, start_totals, jnp.arange(N_DP, dtype=jnp.int32))
    text_gradient, text_loss = totals
    image_gradient = per_block[0].reshape(BATCH, E)
    image_loss = per_block[1].reshape(BATCH)
    image_input, image_weight = tower_back(inputs[0], weights[0], image_unit, image_norm, image_gradient)
    text_input, text_weight = tower_back(inputs[1], weights[1], text_unit, text_norm, text_gradient)
    row_loss = jnp.stack([image_loss, text_loss]) / BATCH
    return (row_loss, jnp.stack([image_input, text_input]), jnp.stack([image_weight, text_weight]))
```

```python
import functools

import jax
import jax.numpy as jnp
from jax import lax
from jax.experimental import pallas as pl
from jax.experimental.pallas import tpu as pltpu
from jax.sharding import PartitionSpec as P

MESH = pl.DeviceIdType.MESH
F32, BF16, I32 = jnp.float32, jnp.bfloat16, jnp.int32
LOGIT_SCALE = 100.0
LOGIT_BIAS = -6.0
NORM_EPS = 1e-06
LOG2E = 1.4426950408889634
LN2 = 0.6931471805599453

E = 1152
Q = 128
H = 64
NT = (((1,), (1,)), ((), ()))


def kernel(x, w, ids, loss_out, dx_out, dw_out, *scratch):
    (
        unit, unit_own, inv_own, part_f, part_own,
        e_send, e_opp, e_recv,
        cols, ring, col_ids, row_ids, sel, xpad, logits, slope, acc, lacc,
        g_send, g_opp, g_recv,
        loss_v, delta, dw_acc, sib_dw, zs_send, zs_recv, x_recv, x_send,
        s_e, r_e, s_i, r_i, s_u, r_u, s_x1, r_x1, s_z1, r_z1, s_z2, r_z2, s_x2, r_x2,
        s_sib, r_sib, s_g, r_g, s_l, r_l, s_d, r_d, s_w, r_w,
    ) = scratch
    t, d, m = lax.axis_index("tower"), lax.axis_index("dp"), lax.axis_index("mp")
    c, z, xh = lax.rem(d, 2), lax.rem(d // 2, 8), d // 16

    def at_dp(xh_, z_, c_):
        return (xh_ * 8 + z_) * 2 + c_

    def zoff(k):
        return lax.rem(z + (k + 8), 8)

    def moff(k):
        return lax.rem(m + (k + 4), 4)

    x_same, x_other = (1 - t, d, m), (1 - t, at_dp(1 - xh, z, c), m)
    z_dev = ((t, at_dp(xh, zoff(1), c), m), (t, at_dp(xh, zoff(-1), c), m))
    y_dev = ((t, d, moff(1)), (t, d, moff(-1)))
    sibling = (t, at_dp(xh, z, 1 - c), m)
    x_far = (t, at_dp(1 - xh, z, c), m)
    others = (x_same, x_other, *z_dev, *y_dev, sibling, x_far)

    sends = []

    def send(src, dst, ss, rs, dev):
        copy = pltpu.make_async_remote_copy(
            src_ref=src, dst_ref=dst, send_sem=ss, recv_sem=rs, device_id=dev, device_id_type=MESH
        )
        copy.start()
        sends.append(copy)

    def recv(dst, rs):
        pltpu.make_async_remote_copy(
            src_ref=dst, dst_ref=dst, send_sem=rs, recv_sem=rs, device_id=sibling, device_id_type=MESH
        ).wait_recv()

    def rows_of(q, lo=0, n=Q):
        return pl.ds(pl.multiple_of(q * Q + lo, 16), n)

    q_opp, q_p, q_m = moff(2), moff(1), moff(-1)
    lo_h, hi_h = pl.ds(0, H), pl.ds(H, H)

    barrier = pltpu.get_barrier_semaphore()
    for dev in others:
        pl.semaphore_signal(barrier, inc=1, device_id=dev, device_id_type=MESH)

    def project(q):
        return jnp.dot(x[rows_of(q), :], w[...], preferred_element_type=F32)

    e_send[0] = project(q_opp).astype(BF16)
    pl.semaphore_wait(barrier, len(others))

    def exchange_opposite(buf, opp, ss, rs):
        send(buf.at[0, lo_h], opp.at[0], ss.at[0], rs.at[0], y_dev[0])
        send(buf.at[0, hi_h], opp.at[1], ss.at[1], rs.at[1], y_dev[1])

    def exchange_direct(k, buf, got, ss, rs):
        half = hi_h if k == 0 else lo_h
        send(buf.at[1 + k, half], got.at[k, half], ss.at[2 + k], rs.at[2 + k], y_dev[k])

    def exchange_sum(k, buf, opp, got, ss, rs, own):
        half = lo_h if k == 0 else hi_h
        recv(opp.at[k], rs.at[k])
        buf[1 + k, half, :] = (own + opp[k].astype(F32)).astype(BF16)
        send(buf.at[1 + k, half], got.at[k, half], ss.at[4 + k], rs.at[4 + k], y_dev[k])

    def exchange_total(got, rs, own):
        for k in range(2):
            recv(got.at[k, hi_h if k == 0 else lo_h], rs.at[2 + k])
            recv(got.at[k, lo_h if k == 0 else hi_h], rs.at[4 + k])
        return own + got[0].astype(F32) + got[1].astype(F32)

    exchange_opposite(e_send, e_opp, s_e, r_e)
    col_ids[z, pl.ds(xh * 2 + c, 1), :] = ids[pl.ds(m, 1), :]
    own_id = col_ids.at[z, pl.ds(xh * 2 + c, 1)]
    send(own_id, own_id, s_i.at[0], r_i.at[0], x_far)
    send(own_id, own_id, s_i.at[1], r_i.at[1], sibling)
    part_f[0] = project(q_p)
    e_send[1, hi_h, :] = part_f[0, hi_h, :].astype(BF16)
    exchange_direct(0, e_send, e_recv, s_e, r_e)
    part_f[1] = project(q_m)
    e_send[2, lo_h, :] = part_f[1, lo_h, :].astype(BF16)
    exchange_direct(1, e_send, e_recv, s_e, r_e)
    part_own[...] = project(m)
    recv(col_ids.at[z, pl.ds((1 - xh) * 2 + c, 1)], r_i.at[0])
    recv(col_ids.at[z, pl.ds(xh * 2 + 1 - c, 1)], r_i.at[1])
    far_id = col_ids.at[z, pl.ds((1 - xh) * 2 + c, 1)]
    send(far_id, far_id, s_i.at[2], r_i.at[2], sibling)
    exchange_sum(0, e_send, e_opp, e_recv, s_e, r_e, part_f[0, lo_h, :])
    exchange_sum(1, e_send, e_opp, e_recv, s_e, r_e, part_f[1, hi_h, :])
    recv(col_ids.at[z, pl.ds((1 - xh) * 2 + 1 - c, 1)], r_i.at[2])

    def ids_ring(s):
        send(col_ids.at[zoff(-s)], col_ids.at[zoff(-s)], s_i.at[3 + 2 * s], r_i.at[3 + 2 * s], z_dev[0])
        if s < 3:
            send(col_ids.at[zoff(s)], col_ids.at[zoff(s)], s_i.at[4 + 2 * s], r_i.at[4 + 2 * s], z_dev[1])

    def ids_wait(s):
        recv(col_ids.at[zoff(-1 - s)], r_i.at[3 + 2 * s])
        if s < 3:
            recv(col_ids.at[zoff(1 + s)], r_i.at[4 + 2 * s])

    ids_ring(0)
    for q in range(4):
        row_ids[pl.ds(q * Q, Q), :] = jnp.transpose(jnp.broadcast_to(ids[pl.ds(q, 1), :], (Q, Q)))
    ids_wait(0)
    ids_ring(1)
    j = lax.broadcasted_iota(I32, (512, 448), 0)
    i = lax.broadcasted_iota(I32, (512, 448), 1)
    r = jnp.bitwise_and(j, 15)
    dest = (
        jnp.bitwise_and(jnp.right_shift(j, 4), 1) * 16
        + jnp.bitwise_and(jnp.right_shift(j, 5), 7) * 2
        + jnp.right_shift(j, 8)
    )
    sel[...] = jnp.where((i == dest * 14 + r) & (r < 14), 1.0, 0.0).astype(BF16)
    ids_wait(1)
    ids_ring(2)
    xpad[...] = lax.dot_general(sel[...], x[...], NT, preferred_element_type=F32).astype(BF16)
    ids_wait(2)
    ids_ring(3)
    acc[...] = jnp.zeros_like(acc)
    lacc[...] = jnp.zeros_like(lacc)
    ids_wait(3)

    emb = exchange_total(e_recv, r_e, part_own[...])
    inv = lax.rsqrt(jnp.sum(emb * emb, axis=1, keepdims=True) + NORM_EPS)
    inv_own[...] = jnp.broadcast_to(inv, (Q, Q))
    uvec = emb * inv
    unit_own[...] = uvec
    unit[rows_of(m), :] = uvec.astype(BF16)

    own_rows = unit.at[rows_of(m)]
    own_lo, own_hi = unit.at[rows_of(m, 0, H)], unit.at[rows_of(m, H, H)]

    def block(z_, xh_, c_, half):
        return cols.at[z_, pl.ds(pl.multiple_of((xh_ * 2 + c_) * Q + half * H, H), H)]

    def ring_send(k, s, src):
        zz = zoff(-s) if k == 0 else zoff(s)
        if s < 3:
            send(src, ring.at[zz], s_z2.at[k, s], r_z2.at[k, s], z_dev[k])
        else:
            part = pl.ds(k * 32, 32)
            send(src.at[part], ring.at[zz, part], s_z2.at[k, s], r_z2.at[k, s], z_dev[k])

    def ring_recv(k, s):
        zz = zoff(-s) if k == 0 else zoff(s)
        if s < 4:
            recv(ring.at[zz], r_z2.at[k, s - 1])
        else:
            part = pl.ds(k * 32, 32)
            recv(ring.at[zz, part], r_z2.at[k, s - 1])

    def across(zz, src):
        dst = block(zz, xh, c, 1)
        send(src, dst, s_x2.at[zz, 0], r_x2.at[zz, 0], x_same)
        send(src, dst, s_x2.at[zz, 1], r_x2.at[zz, 1], x_other)

    def across_recv(zz):
        for k in range(2):
            xk = xh if k == 0 else 1 - xh
            b = block(zz, xk, c, 1)
            recv(b, r_x2.at[zz, k])
            send(b, b, s_sib.at[zz, xk, 1], r_sib.at[zz, xk, 1], sibling)

    def to_sibling(zz, xk):
        b = block(zz, xk, c, 0)
        send(b, b, s_sib.at[zz, xk, 0], r_sib.at[zz, xk, 0], sibling)

    def from_sibling(zz):
        for xk in range(2):
            for half in range(2):
                recv(block(zz, xk, 1 - c, half), r_sib.at[zz, xk, half])

    def z_send(k, s, xk):
        zz = zoff(-s) if k == 0 else zoff(s)
        b = block(zz, xk, c, 0)
        send(b, b, s_z1.at[k, s, xk], r_z1.at[k, s, xk], z_dev[k])

    def z_recv(k, s, xk):
        zz = zoff(-s) if k == 0 else zoff(s)
        recv(block(zz, xk, c, 0), r_z1.at[k, s - 1, xk])

    ring_send(0, 0, own_hi)
    ring_send(1, 0, own_hi)
    send(own_lo, block(z, xh, c, 0), s_x1.at[0], r_x1.at[0], x_same)
    send(own_lo, block(z, xh, c, 0), s_x1.at[1], r_x1.at[1], x_other)
    across(z, own_hi)
    send(own_rows, own_rows, s_u.at[0], r_u.at[0], y_dev[0])
    send(own_rows, own_rows, s_u.at[1], r_u.at[1], y_dev[1])
    for k in range(2):
        xk = xh if k == 0 else 1 - xh
        recv(block(z, xk, c, 0), r_x1.at[k])
    for xk in range(2):
        for k in range(2):
            z_send(k, 0, xk)
        to_sibling(z, xk)
    across_recv(z)
    def pair_unit(zz):
        from_sibling(zz)

        def tile(rt, carry):
            rows = pl.ds(pl.multiple_of(rt * 256, 256), 256)
            logits[...] = lax.dot_general(unit[rows, :], cols[zz], NT, preferred_element_type=F32)

            def chunk(ci, carry):
                lr = pl.ds(pl.multiple_of(ci * 16, 16), 16)
                ar = pl.ds(pl.multiple_of(rt * 256 + ci * 16, 16), 16)
                rid = row_ids[ar, :]
                total = lacc[ar, :]
                for jj in range(4):
                    cc = pl.ds(jj * 128, 128)
                    same = rid == col_ids[zz, pl.ds(jj, 1), :]
                    lg = logits[lr, cc] * (LOGIT_SCALE * LOG2E) + (LOGIT_BIAS * LOG2E)
                    v = jnp.where(same, -lg, lg)
                    e = jnp.exp2(-jnp.abs(v))
                    u = 1.0 + e
                    lg1 = jnp.where(e < 2.0**-12, e * LOG2E, jnp.log2(u))
                    total = total + (jnp.maximum(v, 0.0) + lg1)
                    sg = jnp.where(v >= 0.0, 1.0, e) / u
                    slope[lr, cc] = jnp.where(same, -sg, sg).astype(BF16)
                lacc[ar, :] = total
                return carry

            lax.fori_loop(0, 16, chunk, 0, unroll=2)
            acc[rows, :] += jnp.dot(slope[...], cols[zz], preferred_element_type=F32)
            return carry

        lax.fori_loop(0, 2, tile, 0)

    def pair_units(s):
        if s in (0, 4):
            pair_unit(zoff(s))
        else:
            for k in range(2):
                pair_unit(zoff(s if k else -s))

    for s in range(1, 5):
        ks = range(2)
        for k in ks:
            ring_recv(k, s)
            if s < 4:
                zz = zoff(s if k else -s)
                ring_send(k, s, ring.at[zz])
                across(zz, ring.at[zz])
        if s == 4:
            across(zoff(4), ring.at[zoff(4)])
        for xk in range(2):
            for k in ks:
                if s < 4:
                    z_recv(k, s, xk)
                    if s < 3 or xk == k:
                        z_send(k, s, xk)
                    to_sibling(zoff(s if k else -s), xk)
                elif xk == k:
                    z_recv(k, s, xk)
                    to_sibling(zoff(4), xk)
        if s == 1:
            recv(unit.at[rows_of(q_m)], r_u.at[0])
            fwd = unit.at[rows_of(q_m, 0, H)]
            send(fwd, fwd, s_u.at[2], r_u.at[2], y_dev[0])
            recv(unit.at[rows_of(q_p)], r_u.at[1])
            fwd = unit.at[rows_of(q_p, H, H)]
            send(fwd, fwd, s_u.at[3], r_u.at[3], y_dev[1])
        if s == 2:
            recv(unit.at[rows_of(q_opp, 0, H)], r_u.at[2])
            recv(unit.at[rows_of(q_opp, H, H)], r_u.at[3])
            pair_units(0)
        if s > 1:
            pair_units(s - 1)
        if s < 4:
            across_recv(zoff(-s))
            across_recv(zoff(s))
        else:
            across_recv(zoff(4))
    pair_units(4)

    for q, b in ((q_opp, 0), (q_p, 1), (q_m, 2)):
        if b == 0:
            g_send[0] = acc[rows_of(q), :].astype(BF16)
            exchange_opposite(g_send, g_opp, s_g, r_g)
        else:
            half, lo = (hi_h, H) if b == 1 else (lo_h, 0)
            g_send[b, half, :] = acc[rows_of(q, lo, H), :].astype(BF16)
            exchange_direct(b - 1, g_send, g_recv, s_g, r_g)
    for q in range(4):
        col = jnp.transpose(lacc[pl.ds(q * Q, Q), :])
        loss_v[m, pl.ds(q, 1), :] = jnp.sum(col, axis=0, keepdims=True)
    send(loss_v.at[m], loss_v.at[m], s_l.at[0], r_l.at[0], y_dev[0])
    send(loss_v.at[m], loss_v.at[m], s_l.at[1], r_l.at[1], y_dev[1])
    exchange_sum(0, g_send, g_opp, g_recv, s_g, r_g, acc[rows_of(q_p, 0, H), :])
    exchange_sum(1, g_send, g_opp, g_recv, s_g, r_g, acc[rows_of(q_m, H, H), :])
    recv(loss_v.at[q_m], r_l.at[0])
    send(loss_v.at[q_m], loss_v.at[q_m], s_l.at[2], r_l.at[2], y_dev[0])
    recv(loss_v.at[q_p], r_l.at[1])
    recv(loss_v.at[q_opp], r_l.at[2])
    loss_out[...] = (loss_v[0] + loss_v[1] + loss_v[2] + loss_v[3]) * (LN2 / (512 * 32))
    ug = exchange_total(g_recv, r_g, acc[rows_of(m), :]) * LOGIT_SCALE
    uvec = unit_own[...]
    inner = jnp.sum(uvec * ug, axis=1, keepdims=True)
    delta[rows_of(m), :] = ((ug - uvec * inner) * inv_own[:, 0:1]).astype(BF16)

    def grad_rows(q):
        dx_out[rows_of(q), :] = lax.dot_general(
            delta[rows_of(q), :], w[...], NT, preferred_element_type=F32
        ).astype(BF16)

    own_delta = delta.at[rows_of(m)]
    send(own_delta, own_delta, s_d.at[0], r_d.at[0], y_dev[0])
    send(own_delta, own_delta, s_d.at[1], r_d.at[1], y_dev[1])
    grad_rows(m)
    recv(delta.at[rows_of(q_m)], r_d.at[0])
    fwd = delta.at[rows_of(q_m, 0, H)]
    send(fwd, fwd, s_d.at[2], r_d.at[2], y_dev[0])
    recv(delta.at[rows_of(q_p)], r_d.at[1])
    fwd = delta.at[rows_of(q_p, H, H)]
    send(fwd, fwd, s_d.at[3], r_d.at[3], y_dev[1])
    grad_rows(q_m)
    grad_rows(q_p)
    recv(delta.at[rows_of(q_opp, 0, H)], r_d.at[2])
    recv(delta.at[rows_of(q_opp, H, H)], r_d.at[3])

    for k in range(2):
        cc = 1 - c if k == 0 else c
        rows = pl.ds(pl.multiple_of(cc * 256, 256), 256)
        dw_acc[k] = jnp.dot(xpad[rows, :], delta[...], preferred_element_type=F32)
        if k == 0:
            sib_dw[0] = dw_acc[0].astype(BF16)
            send(sib_dw.at[0], sib_dw.at[1], s_w.at[0], r_w.at[0], sibling)
    grad_rows(q_opp)
    recv(sib_dw.at[1], r_w.at[0])
    dw_acc[1] += sib_dw[1].astype(F32)

    def dest_rows(k, lo=0, n=32):
        return pl.ds(pl.multiple_of(zoff(k) * 32 + lo, 16), n)

    for s in range(4):
        for k in range(2):
            off = (4 - s) if k == 0 else (s - 4)
            if s == 0:
                part = pl.ds(0, 16)
                zs_send[k, 0, part, :] = dw_acc[1, dest_rows(off, 16 * k, 16), :].astype(BF16)
                send(zs_send.at[k, 0, part], zs_recv.at[k, 0, part], s_w.at[1 + k], r_w.at[1 + k], z_dev[k])
                continue
            own = dw_acc[1, dest_rows(off), :]
            if s == 1:
                part = pl.ds(0, 16)
                recv(zs_recv.at[k, 0, part], r_w.at[1 + k])
                got = zs_recv[k, 0, part, :].astype(F32)
                for hx in range(2):
                    v = own[16 * hx : 16 * hx + 16]
                    zs_send[k, 1, pl.ds(16 * hx, 16), :] = (v + got if hx == k else v).astype(BF16)
            else:
                recv(zs_recv.at[k, s - 1], r_w.at[2 * s - 1 + k])
                zs_send[k, s] = (own + zs_recv[k, s - 1].astype(F32)).astype(BF16)
            send(zs_send.at[k, s], zs_recv.at[k, s], s_w.at[2 * s + 1 + k], r_w.at[2 * s + 1 + k], z_dev[k])
    for k in range(2):
        recv(zs_recv.at[k, 3], r_w.at[7 + k])

    def total_rows(xk):
        part = pl.ds(pl.multiple_of(xk * 16, 16), 16)
        return (
            dw_acc[1, pl.ds(pl.multiple_of(z * 32 + xk * 16, 16), 16), :]
            + zs_recv[0, 3, part, :].astype(F32)
            + zs_recv[1, 3, part, :].astype(F32)
        )

    x_send[...] = total_rows(1 - xh).astype(BF16)
    send(x_send, x_recv, s_w.at[9], r_w.at[9], x_far)
    own = total_rows(xh)
    recv(x_recv, r_w.at[9])
    dw_out[...] = (own + x_recv[...].astype(F32))[:14]
    for copy in sends:
        copy.wait_send()


def local(inputs, weights, pair_ids):
    V = pltpu.VMEM
    dma = pltpu.SemaphoreType.DMA
    scratch = [
        V((512, E), BF16), V((Q, E), F32), V((Q, Q), F32), V((2, Q, E), F32), V((Q, E), F32),
        V((3, Q, E), BF16), V((2, H, E), BF16), V((2, Q, E), BF16),
        V((8, 512, E), BF16), V((8, H, E), BF16), V((8, 4, 128), I32), V((512, 128), I32),
        V((512, 448), BF16), V((512, 512), BF16), V((256, 512), F32), V((256, 512), BF16),
        V((512, E), F32), V((512, 128), F32),
        V((3, Q, E), BF16), V((2, H, E), BF16), V((2, Q, E), BF16),
        V((4, 4, 128), F32), V((512, E), BF16), V((2, 256, E), F32), V((2, 256, E), BF16),
        V((2, 4, 32, E), BF16), V((2, 4, 32, E), BF16), V((16, E), BF16), V((16, E), BF16),
    ]
    for shape in (
        (6,), (10,), (4,), (2,), (2, 4, 2), (2, 4), (8, 2), (8, 2, 2), (6,), (3,), (4,), (10,)
    ):
        scratch += [dma(shape), dma(shape)]
    vmem = pl.BlockSpec(memory_space=pltpu.VMEM)
    loss, dx, dw = pl.pallas_call(
        kernel,
        out_shape=(
            jax.ShapeDtypeStruct((4, 128), F32),
            jax.ShapeDtypeStruct((512, 448), BF16),
            jax.ShapeDtypeStruct((14, E), F32),
        ),
        in_specs=[vmem] * 3,
        out_specs=(vmem,) * 3,
        scratch_shapes=scratch,
        compiler_params=pltpu.CompilerParams(
            collective_id=0, has_side_effects=True, vmem_limit_bytes=56 * 2**20
        ),
        cost_estimate=pl.CostEstimate(flops=11 * 10**9, bytes_accessed=2 * 10**6, transcendentals=6 * 10**6),
    )(inputs[0], weights[0], pair_ids.reshape(4, 128))
    return loss.reshape(1, 512), dx[None], dw[None]


def solution(mesh):
    return jax.shard_map(
        local,
        mesh=mesh,
        in_specs=(P("tower", "dp", "mp"), P("tower", "mp", None), P("dp")),
        out_specs=(P("tower", "dp"), P("tower", "dp", "mp"), P("tower", ("mp", "dp"), None)),
        check_vma=False,
    )
```

```python
import jax
import jax.numpy as jnp
from jax import lax
from jax.experimental import pallas as pl
from jax.experimental.pallas import tpu as pltpu
from jax.sharding import PartitionSpec as P

MESH = pl.DeviceIdType.MESH
F32, BF16, I32 = jnp.float32, jnp.bfloat16, jnp.int32
LOGIT_SCALE = 100.0
LOGIT_BIAS = -6.0
NORM_EPS = 1e-06
LOG2E = 1.4426950408889634
LN2 = 0.6931471805599453

E = 1152
Q = 128
H = 64
W = 32
CHUNKS = ((0, 512), (512, 384), (896, 256))
NT = (((1,), (1,)), ((), ()))
TN = (((0,), (0,)), ((), ()))


def kernel(xt, w, ids, loss_out, dx_out, dw_out, *scratch):
    (
        unit, unit_own, inv_own, part_f,
        e_send, e_opp, e_recv,
        cols, ring, col_ids, row_ids, sel, xpad, logits, slope, acc, lacc,
        g_send, g_opp, g_recv,
        loss_v, delta, dw_own, sib_dw, dw_send, dw_recv,
        s_a, s_z, s_x2, s_sib, s_b, s_i, s_l,
        r_e, r_g, r_i, r_u, r_x1, r_z1, r_z2, r_x2, r_sib, r_l, r_d0, r_d1, r_df, r_ws, r_w,
    ) = scratch
    t, d, m = lax.axis_index("tower"), lax.axis_index("dp"), lax.axis_index("mp")
    c, z, xh = lax.rem(d, 2), lax.rem(d // 2, 8), d // 16

    def at_dp(xh_, z_, c_):
        return (xh_ * 8 + z_) * 2 + c_

    def zoff(k):
        return lax.rem(z + (k + 8), 8)

    def moff(k):
        return lax.rem(m + (k + 4), 4)

    x_same, x_other = (1 - t, d, m), (1 - t, at_dp(1 - xh, z, c), m)
    y_dev = ((t, d, moff(1)), (t, d, moff(-1)))
    sibling = (t, at_dp(xh, z, 1 - c), m)
    far = {
        (dz, dx): (t, at_dp(1 - xh if dx else xh, zoff(dz), c), m)
        for dz in range(8) for dx in range(2) if dz or dx
    }
    z_dev = (far[1, 0], far[7, 0])
    x_far = far[0, 1]
    others = (x_same, x_other, *y_dev, sibling, *far.values())

    def send(src, dst, ss, rs, dev):
        pltpu.make_async_remote_copy(
            src_ref=src, dst_ref=dst, send_sem=ss, recv_sem=rs, device_id=dev, device_id_type=MESH
        ).start()

    def share(ref, ss, rs, dev):
        send(ref, ref, ss, rs, dev)

    def recv(dst, rs):
        pltpu.make_async_remote_copy(
            src_ref=dst, dst_ref=dst, send_sem=rs, recv_sem=rs, device_id=sibling, device_id_type=MESH
        ).wait_recv()

    def sent(ref, ss):
        pltpu.make_async_remote_copy(
            src_ref=ref, dst_ref=ref, send_sem=ss, recv_sem=ss, device_id=sibling, device_id_type=MESH
        ).wait_send()

    def rows_of(q, lo=0, n=Q):
        return pl.ds(pl.multiple_of(q * Q + lo, 16), n)

    q_opp, q_p, q_m = moff(2), moff(1), moff(-1)

    barrier = pltpu.get_barrier_semaphore()
    for dev in others:
        pl.semaphore_signal(barrier, inc=1, device_id=dev, device_id_type=MESH)

    def project(q):
        cc = pl.ds(pl.multiple_of(q * Q, Q), Q)
        return lax.dot_general(xt[:, cc], w[...], TN, preferred_element_type=F32)

    e_send[0] = project(q_opp).astype(BF16)
    pl.semaphore_wait(barrier, len(others))

    def part(h, k):
        return pl.ds(h * H + k * W, W)

    def rs_opposite(h, buf, opp, ss, rs):
        for k in range(2):
            send(buf.at[0, part(h, k)], opp.at[h, k], ss, rs.at[h, 0, k], y_dev[k])

    def rs_direct(h, k, buf, got, ss, rs):
        p = part(h, 1 - k)
        send(buf.at[1 + k, p], got.at[k, p], ss, rs.at[h, 1, k], y_dev[k])

    def rs_sum(h, k, buf, opp, got, ss, rs, own):
        p = part(h, k)
        recv(opp.at[h, k], rs.at[h, 0, k])
        buf[1 + k, p, :] = (own + opp[h, k].astype(F32)).astype(BF16)
        send(buf.at[1 + k, p], got.at[k, p], ss, rs.at[h, 2, k], y_dev[k])

    def rs_total(h, got, rs, own):
        for k in range(2):
            recv(got.at[k, part(h, 1 - k)], rs.at[h, 1, k])
            recv(got.at[k, part(h, k)], rs.at[h, 2, k])
        rows = pl.ds(h * H, H)
        return own + got[0, rows, :].astype(F32) + got[1, rows, :].astype(F32)

    def id_row(dc, dx):
        cc = 1 - c if dc else c
        xx = 1 - xh if dx else xh
        return col_ids.at[z, pl.ds(cc * 2 + xx, 1)]

    col_ids[z, pl.ds(c * 2 + xh, 1), :] = ids[pl.ds(m, 1), :]
    share(id_row(0, 0), s_i.at[0], r_i.at[0], x_far)
    share(id_row(0, 0), s_i.at[0], r_i.at[1], sibling)

    def ids_ring(s):
        share(col_ids.at[zoff(-s)], s_i.at[1], r_i.at[3 + 2 * s], z_dev[0])
        if s < 3:
            share(col_ids.at[zoff(s)], s_i.at[1], r_i.at[4 + 2 * s], z_dev[1])

    def ids_wait(s):
        recv(col_ids.at[zoff(-1 - s)], r_i.at[3 + 2 * s])
        if s < 3:
            recv(col_ids.at[zoff(1 + s)], r_i.at[4 + 2 * s])

    for h in range(2):
        rs_opposite(h, e_send, e_opp, s_a, r_e)
    for k, q in ((0, q_p), (1, q_m)):
        part_f[k] = project(q)
        p = part(0, 1 - k)
        e_send[1 + k, p, :] = part_f[k, p, :].astype(BF16)
        rs_direct(0, k, e_send, e_recv, s_a, r_e)
    part_f[2] = project(m)
    for h in range(2):
        if h:
            for k in range(2):
                p = part(1, 1 - k)
                e_send[1 + k, p, :] = part_f[k, p, :].astype(BF16)
                rs_direct(1, k, e_send, e_recv, s_a, r_e)
        for k in range(2):
            rs_sum(h, k, e_send, e_opp, e_recv, s_a, r_e, part_f[k, part(h, k), :])
    recv(id_row(0, 1), r_i.at[0])
    recv(id_row(1, 0), r_i.at[1])
    share(id_row(0, 1), s_i.at[0], r_i.at[2], sibling)

    for q in range(4):
        row_ids[pl.ds(q * Q, Q), :] = jnp.transpose(jnp.broadcast_to(ids[pl.ds(q, 1), :], (Q, Q)))
    j = lax.broadcasted_iota(I32, (512, 448), 0)
    i = lax.broadcasted_iota(I32, (512, 448), 1)
    r = jnp.bitwise_and(j, 15)
    dest = (
        jnp.bitwise_and(jnp.right_shift(j, 4), 1) * 16
        + jnp.bitwise_and(jnp.right_shift(j, 5), 7) * 2
        + jnp.right_shift(j, 8)
    )
    sel[...] = jnp.where((i == dest * 14 + r) & (r < 14), 1.0, 0.0).astype(BF16)
    xpad[...] = jnp.dot(sel[...], xt[...], preferred_element_type=F32).astype(BF16)
    acc[...] = jnp.zeros_like(acc)
    lacc[...] = jnp.zeros_like(lacc)
    recv(id_row(1, 1), r_i.at[2])
    ids_ring(0)

    def normalise(h):
        rows = pl.ds(h * H, H)
        emb = rs_total(h, e_recv, r_e, part_f[2, rows, :])
        inv = lax.rsqrt(jnp.sum(emb * emb, axis=1, keepdims=True) + NORM_EPS)
        inv_own[rows, :] = jnp.broadcast_to(inv, (H, Q))
        uvec = emb * inv
        unit_own[rows, :] = uvec
        unit[rows_of(m, h * H, H), :] = uvec.astype(BF16)

    def block(z_, xh_, c_, half):
        return cols.at[pl.ds(pl.multiple_of(((z_ * 2 + c_) * 2 + xh_) * Q + half * H, H), H)]

    def unit_rows(q, h):
        return unit.at[rows_of(q, h * H, H)]

    def ring_send(k, s, src):
        zz = zoff(-s) if k == 0 else zoff(s)
        if s < 3:
            send(src, ring.at[zz], s_z, r_z2.at[k, s], z_dev[k])
        else:
            p = pl.ds(k * W, W)
            send(src.at[p], ring.at[zz, p], s_z, r_z2.at[k, s], z_dev[k])

    def ring_recv(k, s):
        zz = zoff(-s) if k == 0 else zoff(s)
        if s < 4:
            recv(ring.at[zz], r_z2.at[k, s - 1])
        else:
            recv(ring.at[zz, pl.ds(k * W, W)], r_z2.at[k, s - 1])

    def across(zz, src):
        dst = block(zz, xh, c, 1)
        send(src, dst, s_x2, r_x2.at[zz, 0], x_same)
        send(src, dst, s_x2, r_x2.at[zz, 1], x_other)

    def across_recv(zz):
        for k in range(2):
            b = block(zz, xh if k == 0 else 1 - xh, c, 1)
            recv(b, r_x2.at[zz, k])
            share(b, s_sib, r_sib.at[zz], sibling)

    def to_sibling(zz, xk):
        share(block(zz, xk, c, 0), s_sib, r_sib.at[zz], sibling)

    def z_send(k, s, xk):
        share(block(zoff(-s if k == 0 else s), xk, c, 0), s_z, r_z1.at[k, s, xk], z_dev[k])

    def z_recv(k, s, xk):
        recv(block(zoff(-s if k == 0 else s), xk, c, 0), r_z1.at[k, s - 1, xk])

    normalise(0)
    own = unit_rows(m, 0)
    send(own, block(z, xh, c, 0), s_a, r_x1.at[0], x_same)
    send(own, block(z, xh, c, 0), s_a, r_x1.at[1], x_other)
    for k in range(2):
        share(own, s_a, r_u.at[0, k], y_dev[k])
    ids_wait(0)
    ids_ring(1)
    normalise(1)
    own = unit_rows(m, 1)
    for k in range(2):
        ring_send(k, 0, own)
    across(z, own)
    for k in range(2):
        share(own, s_a, r_u.at[1, k], y_dev[k])
    ids_wait(1)
    ids_ring(2)
    for k in range(2):
        recv(block(z, xh if k == 0 else 1 - xh, c, 0), r_x1.at[k])
    for xk in range(2):
        for k in range(2):
            z_send(k, 0, xk)
    for xk in range(2):
        to_sibling(z, xk)

    def pair_tile(zz, start, n):
        rows = pl.ds(pl.multiple_of(start, n), n)
        cc = pl.ds(pl.multiple_of(zz * 512, 512), 512)
        lr_all = pl.ds(0, n)
        logits[lr_all, :] = lax.dot_general(unit[rows, :], cols[cc, :], NT, preferred_element_type=F32)

        def chunk(ci, carry):
            lr = pl.ds(pl.multiple_of(ci * 16, 16), 16)
            ar = pl.ds(pl.multiple_of(start + ci * 16, 16), 16)
            rid = row_ids[ar, :]
            total = lacc[ar, :]
            for jj in range(4):
                lc = pl.ds(jj * 128, 128)
                same = rid == col_ids[zz, pl.ds(jj, 1), :]
                lg = logits[lr, lc] * (LOGIT_SCALE * LOG2E) + (LOGIT_BIAS * LOG2E)
                v = jnp.where(same, -lg, lg)
                e = jnp.exp2(-jnp.abs(v))
                u = 1.0 + e
                lg1 = jnp.where(e < 2.0**-12, e * LOG2E, jnp.log2(u))
                total = total + (jnp.maximum(v, 0.0) + lg1)
                sg = jnp.where(v >= 0.0, 1.0, e) / u
                slope[lr, lc] = jnp.where(same, -sg, sg).astype(BF16)
            lacc[ar, :] = total
            return carry

        lax.fori_loop(0, n // 16, chunk, 0, unroll=2)
        acc[rows, :] += jnp.dot(slope[lr_all, :], cols[cc, :], preferred_element_type=F32)

    def from_sibling(zz):
        rows = pl.ds(pl.multiple_of((zz * 2 + 1 - c) * 2 * Q, 2 * Q), 2 * Q)
        recv(cols.at[rows], r_sib.at[zz])

    done = [0]

    def tiles(n):
        def tile(ti, carry):
            u, rt = ti // 2, lax.rem(ti, 2)
            dist = (u + 1) // 2
            zz = lax.rem(z + jnp.where(lax.rem(u, 2) == 1, dist, 8 - dist), 8)

            @pl.when(rt == 0)
            def _():
                from_sibling(zz)

            pair_tile(zz, rt * 256, 256)
            return carry

        lax.fori_loop(done[0], done[0] + n, tile, 0)
        done[0] += n

    slots = {2: (2, 2, 1, 1), 3: (1, 1, 1, 1), 4: (2, 1, 1, 0)}
    for s in range(1, 5):
        dist = (s,) if s == 4 else (-s, s)
        run = slots.get(s, (0, 0, 0, 0))
        if s < 3:
            ids_wait(s + 1)
            if s == 1:
                ids_ring(3)
        for k in range(2):
            ring_recv(k, s)
            if s < 4:
                ring_send(k, s, ring.at[zoff(dist[k])])
        for ds_ in dist:
            across(zoff(ds_), ring.at[zoff(ds_)])
        if s == 1:
            across_recv(z)
            recv(unit_rows(q_m, 0), r_u.at[0, 0])
            share(unit_rows(q_m, 0), s_a, r_u.at[2, 0], y_dev[0])
            recv(unit_rows(q_p, 0), r_u.at[0, 1])
        if s == 2:
            recv(unit_rows(q_m, 1), r_u.at[1, 0])
            recv(unit_rows(q_opp, 0), r_u.at[2, 0])
            recv(unit_rows(q_opp, 1), r_u.at[2, 1])
        if run[0]:
            tiles(run[0])
        for xk in range(2):
            for k in range(2):
                if s < 4:
                    z_recv(k, s, xk)
                    if s < 3 or xk == k:
                        z_send(k, s, xk)
                elif xk == k:
                    z_recv(k, s, xk)
            for k in range(len(dist)):
                to_sibling(zoff(dist[k]), xk)
            if run[1 + xk]:
                tiles(run[1 + xk])
            if s == 1 and xk == 0:
                recv(unit_rows(q_p, 1), r_u.at[1, 1])
                share(unit_rows(q_p, 1), s_a, r_u.at[2, 1], y_dev[1])
        for ds_ in dist:
            across_recv(zoff(ds_))
        if run[3]:
            tiles(run[3])

    z_last = zoff(4)
    from_sibling(z_last)
    pair_tile(z_last, q_opp * Q, Q)
    g_send[0] = acc[rows_of(q_opp), :].astype(BF16)
    for h in range(2):
        rs_opposite(h, g_send, g_opp, s_b, r_g)
    for k, q in ((0, q_p), (1, q_m)):
        pair_tile(z_last, q * Q, Q)
        g_send[1 + k, part(0, 1 - k), :] = acc[rows_of(q, (1 - k) * W, W), :].astype(BF16)
        rs_direct(0, k, g_send, g_recv, s_b, r_g)
    pair_tile(z_last, m * Q, Q)
    for q in range(4):
        col = jnp.transpose(lacc[pl.ds(q * Q, Q), :])
        loss_v[m, pl.ds(q, 1), :] = jnp.sum(col, axis=0, keepdims=True)
    for h in range(2):
        if h:
            for k, q in ((0, q_p), (1, q_m)):
                g_send[1 + k, part(1, 1 - k), :] = acc[rows_of(q, H + (1 - k) * W, W), :].astype(BF16)
                rs_direct(1, k, g_send, g_recv, s_b, r_g)
        for k, q in ((0, q_p), (1, q_m)):
            rs_sum(h, k, g_send, g_opp, g_recv, s_b, r_g, acc[rows_of(q, h * H + k * W, W), :])
    for k in range(2):
        share(loss_v.at[m], s_l, r_l.at[k], y_dev[k])

    def back(h):
        rows = pl.ds(h * H, H)
        ug = rs_total(h, g_recv, r_g, acc[rows_of(m, h * H, H), :]) * LOGIT_SCALE
        uvec = unit_own[rows, :]
        inner = jnp.sum(uvec * ug, axis=1, keepdims=True)
        delta[rows_of(m, h * H, H), :] = ((ug - uvec * inner) * inv_own[rows, 0:1]).astype(BF16)

    def delta_rows(q, h, e=None):
        rows = rows_of(q, h * H, H)
        return delta.at[rows] if e is None else delta.at[rows, pl.ds(*CHUNKS[e])]

    def grad_rows(q):
        dx_out[:, pl.ds(pl.multiple_of(q * Q, Q), Q)] = lax.dot_general(
            w[...], delta[rows_of(q), :], NT, preferred_element_type=F32
        ).astype(BF16)

    back(0)
    for k in range(2):
        share(delta_rows(m, 0), s_b, r_d0.at[k], y_dev[k])
    back(1)
    for e in range(3):
        for k in range(2):
            share(delta_rows(m, 1, e), s_b, r_d1.at[k, e], y_dev[k])
    grad_rows(m)
    recv(delta_rows(q_m, 0), r_d0.at[0])
    for e in range(3):
        share(delta_rows(q_m, 0, e), s_b, r_df.at[0, e], y_dev[0])
    recv(loss_v.at[q_m], r_l.at[0])
    share(loss_v.at[q_m], s_l, r_l.at[2], y_dev[0])
    for e in range(3):
        recv(delta_rows(q_p, 1, e), r_d1.at[1, e])
        share(delta_rows(q_p, 1, e), s_b, r_df.at[1, e], y_dev[1])
    recv(delta_rows(q_p, 0), r_d0.at[1])
    grad_rows(q_p)
    for e in range(3):
        recv(delta_rows(q_m, 1, e), r_d1.at[0, e])
    grad_rows(q_m)

    def dw_products(e):
        cc = pl.ds(*CHUNKS[e])
        recv(delta_rows(q_opp, 0, e), r_df.at[0, e])
        recv(delta_rows(q_opp, 1, e), r_df.at[1, e])
        for dc in range(2):
            rows = pl.ds(pl.multiple_of((c if dc else 1 - c) * 256, 256), 256)
            prod = jnp.dot(xpad[rows, :], delta[:, cc], preferred_element_type=F32)
            if dc:
                dw_own[:, cc] = prod
            else:
                sib_dw[0, :, cc] = prod.astype(BF16)
                send(sib_dw.at[0, :, cc], sib_dw.at[1, :, cc], s_b, r_ws.at[e], sibling)

    def dest_rows(dz, dx):
        xx = 1 - xh if dx else xh
        return pl.ds(pl.multiple_of((zoff(dz) * 2 + xx) * 16, 16), 16)

    def dw_exchange(e):
        cc = pl.ds(*CHUNKS[e])
        recv(sib_dw.at[1, :, cc], r_ws.at[e])
        both = dw_own[:, cc] + sib_dw[1, :, cc].astype(F32)
        dw_own[:, cc] = both
        dw_send[:, cc] = both.astype(BF16)
        for n, (dz, dx) in enumerate(far):
            send(
                dw_send.at[dest_rows(dz, dx), cc], dw_recv.at[pl.ds(n * 16, 16), cc],
                s_b, r_w.at[e], far[dz, dx],
            )

    dw_products(0)
    dw_products(1)
    dw_exchange(0)
    dw_products(2)
    dw_exchange(1)
    dw_exchange(2)
    grad_rows(q_opp)
    recv(loss_v.at[q_p], r_l.at[1])
    recv(loss_v.at[q_opp], r_l.at[2])
    loss = (loss_v[0] + loss_v[1] + loss_v[2] + loss_v[3]) * (LN2 / (512 * 32))
    for q in range(4):
        loss_out[:, pl.ds(q * Q, Q)] = loss[q : q + 1]
    for e in range(3):
        cc = pl.ds(*CHUNKS[e])
        recv(dw_recv.at[:, cc], r_w.at[e])
        total = dw_own[dest_rows(0, 0), cc]
        for n in range(15):
            total = total + dw_recv[pl.ds(n * 16, 16), cc].astype(F32)
        for row in range(14):
            dw_out[row, :, cc] = total[row : row + 1]
    for ss, n in ((s_a, 384 + 128 + 384), (s_z, 14 * 64 + 448), (s_x2, 1024), (s_sib, 2048), (s_b, 384 + 384 + 256 + 240)):
        sent(cols.at[pl.ds(0, n)], ss)
    sent(col_ids.at[0, pl.ds(0, 3)], s_i.at[0])
    sent(col_ids.at[pl.ds(0, 7)], s_i.at[1])
    sent(loss_v.at[pl.ds(0, 3)], s_l)


def local(inputs, weights, pair_ids):
    V = pltpu.VMEM
    dma = pltpu.SemaphoreType.DMA
    scratch = [
        V((512, E), BF16), V((Q, E), F32), V((Q, Q), F32), V((3, Q, E), F32),
        V((3, Q, E), BF16), V((2, 2, W, E), BF16), V((2, Q, E), BF16),
        V((4096, E), BF16), V((8, H, E), BF16), V((8, 4, 128), I32), V((512, 128), I32),
        V((512, 448), BF16), V((512, 512), BF16), V((256, 512), F32), V((256, 512), BF16),
        V((512, E), F32), V((512, 128), F32),
        V((3, Q, E), BF16), V((2, 2, W, E), BF16), V((2, Q, E), BF16),
        V((4, 4, 128), F32), V((512, E), BF16), V((256, E), F32), V((2, 256, E), BF16),
        V((256, E), BF16), V((240, E), BF16),
    ]
    for shape in (
        (), (), (), (), (), (2,), (),
        (2, 3, 2), (2, 3, 2), (10,), (3, 2), (2,), (2, 4, 2), (2, 4), (8, 2), (8,), (3,),
        (2,), (2, 3), (2, 3), (3,), (3,),
    ):
        scratch.append(dma(shape))
    vmem = pl.BlockSpec(memory_space=pltpu.VMEM)
    loss, dx, dw = pl.pallas_call(
        kernel,
        out_shape=(
            jax.ShapeDtypeStruct((1, 512), F32),
            jax.ShapeDtypeStruct((448, 512), BF16),
            jax.ShapeDtypeStruct((14, 1, E), F32),
        ),
        in_specs=[vmem] * 3,
        out_specs=(vmem,) * 3,
        scratch_shapes=scratch,
        compiler_params=pltpu.CompilerParams(
            collective_id=0, has_side_effects=True, vmem_limit_bytes=56 * 2**20
        ),
        cost_estimate=pl.CostEstimate(flops=11 * 10**9, bytes_accessed=2 * 10**6, transcendentals=6 * 10**6),
    )(jnp.swapaxes(inputs[0], 0, 1), weights[0], pair_ids.reshape(4, 128))
    return loss, jnp.swapaxes(dx, 0, 1)[None], dw.reshape(1, 14, E)


def solution(mesh):
    return jax.shard_map(
        local,
        mesh=mesh,
        in_specs=(P("tower", "dp", "mp"), P("tower", "mp", None), P("dp")),
        out_specs=(P("tower", "dp"), P("tower", "dp", "mp"), P("tower", ("mp", "dp"), None)),
        check_vma=False,
    )
```

```python
import jax
import jax.numpy as jnp
from jax import lax
from jax.experimental import pallas as pl
from jax.experimental.pallas import tpu as pltpu
from jax.sharding import PartitionSpec as P

MESH = pl.DeviceIdType.MESH
F32, BF16, I32 = jnp.float32, jnp.bfloat16, jnp.int32
LOGIT_SCALE = 100.0
LOGIT_BIAS = -6.0
NORM_EPS = 1e-06
LOG2E = 1.4426950408889634
LN2 = 0.6931471805599453

E = 1152
Q = 128
H = 64
W = 32
V = 16
CHUNKS = ((0, 384), (384, 384), (768, 384))
NT = (((1,), (1,)), ((), ()))
TN = (((0,), (0,)), ((), ()))


def kernel(xt, w, ids, loss_out, dx_out, dw_out, *scratch):
    (
        unit, unit_own, inv_own, part_f,
        e_send, e_opp, e_recv,
        cols, ring, col_ids, row_ids, sel, xpad, logits, slope, acc, lacc,
        g_send, g_opp, g_recv,
        loss_v, delta, dw_own, sib_dw, dw_send, dw_recv, dx_recv,
        s_a, s_z, s_x2, s_sib, s_b, s_i, s_l,
        r_e, r_g, r_i, r_u, r_x1, r_z0, r_z1, r_z2, r_x2, r_sib, r_l, r_d0, r_d1, r_df, r_ws, r_wx, r_w,
    ) = scratch
    t, d, m = lax.axis_index("tower"), lax.axis_index("dp"), lax.axis_index("mp")
    c, z, xh = lax.rem(d, 2), lax.rem(d // 2, 8), d // 16

    def at_dp(xh_, z_, c_):
        return (xh_ * 8 + z_) * 2 + c_

    def zoff(k):
        return lax.rem(z + (k + 8), 8)

    def moff(k):
        return lax.rem(m + (k + 4), 4)

    x_same, x_other = (1 - t, d, m), (1 - t, at_dp(1 - xh, z, c), m)
    y_dev = ((t, d, moff(1)), (t, d, moff(-1)))
    sibling = (t, at_dp(xh, z, 1 - c), m)
    far = {
        (dz, dx): (t, at_dp(1 - xh if dx else xh, zoff(dz), c), m)
        for dx in range(2) for dz in range(8) if dz or dx
    }
    z_dev = (far[1, 0], far[7, 0])
    x_far = far[0, 1]
    others = (x_same, x_other, *y_dev, sibling, *far.values())

    def send(src, dst, ss, rs, dev):
        pltpu.make_async_remote_copy(
            src_ref=src, dst_ref=dst, send_sem=ss, recv_sem=rs, device_id=dev, device_id_type=MESH
        ).start()

    def share(ref, ss, rs, dev):
        send(ref, ref, ss, rs, dev)

    def recv(dst, rs):
        pltpu.make_async_remote_copy(
            src_ref=dst, dst_ref=dst, send_sem=rs, recv_sem=rs, device_id=sibling, device_id_type=MESH
        ).wait_recv()

    def sent(ref, ss):
        pltpu.make_async_remote_copy(
            src_ref=ref, dst_ref=ref, send_sem=ss, recv_sem=ss, device_id=sibling, device_id_type=MESH
        ).wait_send()

    def rows_of(q, lo=0, n=Q):
        return pl.ds(pl.multiple_of(q * Q + lo, 16), n)

    q_opp, q_p, q_m = moff(2), moff(1), moff(-1)

    barrier = pltpu.get_barrier_semaphore()
    for dev in others:
        pl.semaphore_signal(barrier, inc=1, device_id=dev, device_id_type=MESH)

    def project(q):
        cc = pl.ds(pl.multiple_of(q * Q, Q), Q)
        return lax.dot_general(xt[:, cc], w[...], TN, preferred_element_type=F32)

    e_send[0] = project(q_opp).astype(BF16)
    pl.semaphore_wait(barrier, len(others))

    def part(h, k, n):
        return pl.ds((2 * h + k) * n, n)

    def rs_opposite(h, buf, opp, ss, rs):
        n = opp.shape[2]
        for k in range(2):
            send(buf.at[0, part(h, k, n)], opp.at[h, k], ss, rs.at[h, 0, k], y_dev[k])

    def rs_direct(h, k, buf, got, ss, rs, n):
        p = part(h, 1 - k, n)
        send(buf.at[1 + k, p], got.at[k, p], ss, rs.at[h, 1, k], y_dev[k])

    def rs_sum(h, k, buf, opp, got, ss, rs, own):
        p = part(h, k, opp.shape[2])
        recv(opp.at[h, k], rs.at[h, 0, k])
        buf[1 + k, p, :] = (own + opp[h, k].astype(F32)).astype(BF16)
        send(buf.at[1 + k, p], got.at[k, p], ss, rs.at[h, 2, k], y_dev[k])

    def rs_total(h, got, rs, own, n):
        for k in range(2):
            recv(got.at[k, part(h, 1 - k, n)], rs.at[h, 1, k])
            recv(got.at[k, part(h, k, n)], rs.at[h, 2, k])
        rows = pl.ds(2 * h * n, 2 * n)
        return own + got[0, rows, :].astype(F32) + got[1, rows, :].astype(F32)

    def id_row(dc, dx):
        cc = 1 - c if dc else c
        xx = 1 - xh if dx else xh
        return col_ids.at[z, pl.ds(cc * 2 + xx, 1)]

    col_ids[z, pl.ds(c * 2 + xh, 1), :] = ids[pl.ds(m, 1), :]
    share(id_row(0, 0), s_i.at[0], r_i.at[0], x_far)
    share(id_row(0, 0), s_i.at[0], r_i.at[1], sibling)

    def ids_ring(s):
        share(col_ids.at[zoff(-s)], s_i.at[1], r_i.at[3 + 2 * s], z_dev[0])
        if s < 3:
            share(col_ids.at[zoff(s)], s_i.at[1], r_i.at[4 + 2 * s], z_dev[1])

    def ids_wait(s):
        recv(col_ids.at[zoff(-1 - s)], r_i.at[3 + 2 * s])
        if s < 3:
            recv(col_ids.at[zoff(1 + s)], r_i.at[4 + 2 * s])

    for h in range(4):
        rs_opposite(h, e_send, e_opp, s_a, r_e)
    for k, q in ((0, q_p), (1, q_m)):
        part_f[k] = project(q)
    for h in range(4):
        for k in range(2):
            p = part(h, 1 - k, V)
            e_send[1 + k, p, :] = part_f[k, p, :].astype(BF16)
            rs_direct(h, k, e_send, e_recv, s_a, r_e, V)
        for k in range(2):
            rs_sum(h, k, e_send, e_opp, e_recv, s_a, r_e, part_f[k, part(h, k, V), :])
    part_f[2] = project(m)
    recv(id_row(0, 1), r_i.at[0])
    recv(id_row(1, 0), r_i.at[1])
    share(id_row(0, 1), s_i.at[0], r_i.at[2], sibling)

    for q in range(4):
        row_ids[pl.ds(q * Q, Q), :] = jnp.transpose(jnp.broadcast_to(ids[pl.ds(q, 1), :], (Q, Q)))
    j = lax.broadcasted_iota(I32, (512, 448), 0)
    i = lax.broadcasted_iota(I32, (512, 448), 1)
    r = jnp.bitwise_and(j, 15)
    dest = (
        jnp.bitwise_and(jnp.right_shift(j, 7), 1) * 16
        + jnp.bitwise_and(jnp.right_shift(j, 4), 7) * 2
        + jnp.right_shift(j, 8)
    )
    sel[...] = jnp.where((i == dest * 14 + r) & (r < 14), 1.0, 0.0).astype(BF16)
    xpad[...] = jnp.dot(sel[...], xt[...], preferred_element_type=F32).astype(BF16)
    acc[...] = jnp.zeros_like(acc)
    lacc[...] = jnp.zeros_like(lacc)
    recv(id_row(1, 1), r_i.at[2])
    ids_ring(0)

    def normalise(h):
        rows = pl.ds(h * W, W)
        emb = rs_total(h, e_recv, r_e, part_f[2, rows, :], V)
        inv = lax.rsqrt(jnp.sum(emb * emb, axis=1, keepdims=True) + NORM_EPS)
        inv_own[rows, :] = jnp.broadcast_to(inv, (W, Q))
        uvec = emb * inv
        unit_own[rows, :] = uvec
        unit[rows_of(m, h * W, W), :] = uvec.astype(BF16)

    def block(z_, xh_, c_, lo, n):
        return cols.at[pl.ds(pl.multiple_of(((z_ * 2 + c_) * 2 + xh_) * Q + lo, 16), n)]

    def unit_rows(q, h):
        return unit.at[rows_of(q, h * H, H)]

    def ring_send(k, s, p, src):
        if s < 3 or p == k:
            zz = zoff(-s if k == 0 else s)
            send(src, ring.at[zz, pl.ds(p * W, W)], s_z, r_z2.at[k, s, p], z_dev[k])

    def ring_recv(k, s, p):
        zz = zoff(-s if k == 0 else s)
        piece = ring.at[zz, pl.ds(p * W, W)]
        if s < 4 or p == k:
            recv(piece, r_z2.at[k, s - 1, p])
        if s < 4:
            ring_send(k, s, p, piece)

    def across(zz, src):
        dst = block(zz, xh, c, 0, H)
        send(src, dst, s_x2, r_x2.at[zz, 0], x_same)
        send(src, dst, s_x2, r_x2.at[zz, 1], x_other)

    def across_recv(zz):
        for k in range(2):
            b = block(zz, xh if k == 0 else 1 - xh, c, 0, H)
            recv(b, r_x2.at[zz, k])
            share(b, s_sib, r_sib.at[zz], sibling)

    def to_sibling(zz, xk):
        share(block(zz, xk, c, H, H), s_sib, r_sib.at[zz], sibling)

    def z_first(p):
        for k in range(2):
            recv(block(z, xh if k == 0 else 1 - xh, c, H + p * W, W), r_x1.at[k, p])
        for xk in range(2):
            for k in range(2):
                share(block(z, xk, c, H + p * W, W), s_z, r_z0.at[k, xk, p], z_dev[k])

    def z_send(k, s, xk):
        share(block(zoff(-s if k == 0 else s), xk, c, H, H), s_z, r_z1.at[k, s - 1, xk], z_dev[k])

    def z_recv(k, s, xk):
        zz = zoff(-s if k == 0 else s)
        if s == 1:
            for p in range(2):
                recv(block(zz, xk, c, H + p * W, W), r_z0.at[k, xk, p])
        else:
            recv(block(zz, xk, c, H, H), r_z1.at[k, s - 2, xk])

    for h in range(4):
        normalise(h)
        own = unit.at[rows_of(m, h * W, W)]
        if h < 2:
            for k in range(2):
                ring_send(k, 0, h, own)
        else:
            dst = block(z, xh, c, h * W, W)
            send(own, dst, s_a, r_x1.at[0, h - 2], x_same)
            send(own, dst, s_a, r_x1.at[1, h - 2], x_other)
        if h % 2:
            for k in range(2):
                share(unit_rows(m, h // 2), s_a, r_u.at[h // 2, k], y_dev[k])
            ids_wait(h // 2)
            ids_ring(h // 2 + 1)
    across(z, unit_rows(m, 0))
    for p in range(2):
        for k in range(2):
            ring_recv(k, 1, p)
    for p in range(2):
        z_first(p)
    for xk in range(2):
        to_sibling(z, xk)

    def pair_tile(zz, start, n):
        rows = pl.ds(pl.multiple_of(start, n), n)
        cc = pl.ds(pl.multiple_of(zz * 512, 512), 512)
        lr_all = pl.ds(0, n)
        logits[lr_all, :] = lax.dot_general(unit[rows, :], cols[cc, :], NT, preferred_element_type=F32)

        def chunk(ci, carry):
            lr = pl.ds(pl.multiple_of(ci * 16, 16), 16)
            ar = pl.ds(pl.multiple_of(start + ci * 16, 16), 16)
            rid = row_ids[ar, :]
            total = lacc[ar, :]
            for jj in range(4):
                lc = pl.ds(jj * 128, 128)
                same = rid == col_ids[zz, pl.ds(jj, 1), :]
                lg = logits[lr, lc] * (LOGIT_SCALE * LOG2E) + (LOGIT_BIAS * LOG2E)
                v = jnp.where(same, -lg, lg)
                e = jnp.exp2(-jnp.abs(v))
                u = 1.0 + e
                lg1 = jnp.where(e < 2.0**-12, e * LOG2E, jnp.log2(u))
                total = total + (jnp.maximum(v, 0.0) + lg1)
                sg = jnp.where(v >= 0.0, 1.0, e) / u
                slope[lr, lc] = jnp.where(same, -sg, sg).astype(BF16)
            lacc[ar, :] = total
            return carry

        lax.fori_loop(0, n // 16, chunk, 0, unroll=2)
        acc[rows, :] += jnp.dot(slope[lr_all, :], cols[cc, :], preferred_element_type=F32)

    def from_sibling(zz):
        rows = pl.ds(pl.multiple_of((zz * 2 + 1 - c) * 2 * Q, 2 * Q), 2 * Q)
        recv(cols.at[rows], r_sib.at[zz])

    done = [0]

    def tiles(n):
        def tile(ti, carry):
            u, rt = ti // 2, lax.rem(ti, 2)
            dist = (u + 1) // 2
            zz = lax.rem(z + jnp.where(lax.rem(u, 2) == 1, dist, 8 - dist), 8)

            @pl.when(rt == 0)
            def _():
                from_sibling(zz)

            pair_tile(zz, rt * 256, 256)
            return carry

        lax.fori_loop(done[0], done[0] + n, tile, 0)
        done[0] += n

    slots = {2: (2, 2, 1, 1), 3: (1, 1, 1, 1), 4: (2, 1, 1, 0)}
    for s in range(1, 5):
        dist = (s,) if s == 4 else (-s, s)
        run = slots.get(s, (0, 0, 0, 0))
        if s < 3:
            ids_wait(s + 1)
            if s == 1:
                ids_ring(3)
        if s > 1:
            for p in range(2):
                for k in range(2):
                    ring_recv(k, s, p)
        for ds_ in dist:
            across(zoff(ds_), ring.at[zoff(ds_)])
        if s == 1:
            across_recv(z)
            recv(unit_rows(q_m, 0), r_u.at[0, 0])
            share(unit_rows(q_m, 0), s_a, r_u.at[2, 0], y_dev[0])
            recv(unit_rows(q_p, 0), r_u.at[0, 1])
        if s == 2:
            recv(unit_rows(q_m, 1), r_u.at[1, 0])
            recv(unit_rows(q_opp, 0), r_u.at[2, 0])
            recv(unit_rows(q_opp, 1), r_u.at[2, 1])
        if run[0]:
            tiles(run[0])
        for xk in range(2):
            for k in range(2):
                if s < 4:
                    z_recv(k, s, xk)
                    if s < 3 or xk == k:
                        z_send(k, s, xk)
                elif xk == k:
                    z_recv(k, s, xk)
            for k in range(len(dist)):
                to_sibling(zoff(dist[k]), xk)
            if run[1 + xk]:
                tiles(run[1 + xk])
            if s == 1 and xk == 0:
                recv(unit_rows(q_p, 1), r_u.at[1, 1])
                share(unit_rows(q_p, 1), s_a, r_u.at[2, 1], y_dev[1])
        for ds_ in dist:
            across_recv(zoff(ds_))
        if run[3]:
            tiles(run[3])

    z_last = zoff(4)
    from_sibling(z_last)
    pair_tile(z_last, q_opp * Q, Q)
    g_send[0] = acc[rows_of(q_opp), :].astype(BF16)
    for h in range(2):
        rs_opposite(h, g_send, g_opp, s_b, r_g)
    for k, q in ((0, q_p), (1, q_m)):
        pair_tile(z_last, q * Q, Q)
        g_send[1 + k, part(0, 1 - k, W), :] = acc[rows_of(q, (1 - k) * W, W), :].astype(BF16)
        rs_direct(0, k, g_send, g_recv, s_b, r_g, W)
    pair_tile(z_last, m * Q, Q)
    for q in range(4):
        col = jnp.transpose(lacc[pl.ds(q * Q, Q), :])
        loss_v[m, pl.ds(q, 1), :] = jnp.sum(col, axis=0, keepdims=True)
    for h in range(2):
        if h:
            for k, q in ((0, q_p), (1, q_m)):
                g_send[1 + k, part(1, 1 - k, W), :] = acc[rows_of(q, H + (1 - k) * W, W), :].astype(BF16)
                rs_direct(1, k, g_send, g_recv, s_b, r_g, W)
        for k, q in ((0, q_p), (1, q_m)):
            rs_sum(h, k, g_send, g_opp, g_recv, s_b, r_g, acc[rows_of(q, h * H + k * W, W), :])
    for k in range(2):
        share(loss_v.at[m], s_l, r_l.at[k], y_dev[k])

    def back(h):
        rows = pl.ds(h * H, H)
        ug = rs_total(h, g_recv, r_g, acc[rows_of(m, h * H, H), :], W) * LOGIT_SCALE
        uvec = unit_own[rows, :]
        inner = jnp.sum(uvec * ug, axis=1, keepdims=True)
        delta[rows_of(m, h * H, H), :] = ((ug - uvec * inner) * inv_own[rows, 0:1]).astype(BF16)

    def delta_rows(q, h, e=None):
        rows = rows_of(q, h * H, H)
        return delta.at[rows] if e is None else delta.at[rows, pl.ds(*CHUNKS[e])]

    def grad_rows(q):
        dx_out[:, pl.ds(pl.multiple_of(q * Q, Q), Q)] = lax.dot_general(
            w[...], delta[rows_of(q), :], NT, preferred_element_type=F32
        ).astype(BF16)

    back(0)
    for k in range(2):
        share(delta_rows(m, 0), s_b, r_d0.at[k], y_dev[k])
    back(1)
    for e in range(3):
        for k in range(2):
            share(delta_rows(m, 1, e), s_b, r_d1.at[k, e], y_dev[k])
    grad_rows(m)
    recv(delta_rows(q_m, 0), r_d0.at[0])
    for e in range(3):
        share(delta_rows(q_m, 0, e), s_b, r_df.at[0, e], y_dev[0])
    recv(loss_v.at[q_m], r_l.at[0])
    share(loss_v.at[q_m], s_l, r_l.at[2], y_dev[0])
    for e in range(3):
        recv(delta_rows(q_p, 1, e), r_d1.at[1, e])
        share(delta_rows(q_p, 1, e), s_b, r_df.at[1, e], y_dev[1])
    recv(delta_rows(q_p, 0), r_d0.at[1])
    grad_rows(q_p)
    for e in range(3):
        recv(delta_rows(q_m, 1, e), r_d1.at[0, e])
    grad_rows(q_m)

    def dw_products(e):
        cc = pl.ds(*CHUNKS[e])
        recv(delta_rows(q_opp, 0, e), r_df.at[0, e])
        recv(delta_rows(q_opp, 1, e), r_df.at[1, e])
        for dc in range(2):
            rows = pl.ds(pl.multiple_of((c if dc else 1 - c) * 256, 256), 256)
            prod = jnp.dot(xpad[rows, :], delta[:, cc], preferred_element_type=F32)
            if dc:
                dw_own[:, cc] = prod
            else:
                sib_dw[0, :, cc] = prod.astype(BF16)
                send(sib_dw.at[0, :, cc], sib_dw.at[1, :, cc], s_b, r_ws.at[e], sibling)

    def x_rows(dx):
        return pl.ds(pl.multiple_of((1 - xh if dx else xh) * 128, 128), 128)

    def dest_rows(dz, dx):
        return pl.ds(pl.multiple_of(((1 - xh if dx else xh) * 8 + zoff(dz)) * 16, 16), 16)

    slots_of = {dest: pl.ds(n * 16, 16) for n, dest in enumerate(far)}

    def dw_cores(e):
        cc = pl.ds(*CHUNKS[e])
        recv(sib_dw.at[1, :, cc], r_ws.at[e])
        both = dw_own[:, cc] + sib_dw[1, :, cc].astype(F32)
        dw_own[:, cc] = both
        dw_send[:, cc] = both.astype(BF16)
        if e < 2:
            send(dw_send.at[x_rows(1), cc], dx_recv.at[:, cc], s_b, r_wx.at[e], x_far)
        else:
            dw_out_of(e, far)

    def dw_x(e):
        cc = pl.ds(*CHUNKS[e])
        recv(dx_recv.at[:, cc], r_wx.at[e])
        both = dw_own[x_rows(0), cc] + dx_recv[:, cc].astype(F32)
        dw_own[x_rows(0), cc] = both
        dw_send[x_rows(0), cc] = both.astype(BF16)
        dw_out_of(e, [dest for dest in far if not dest[1]])

    def dw_out_of(e, dests):
        cc = pl.ds(*CHUNKS[e])
        for dest in dests:
            send(dw_send.at[dest_rows(*dest), cc], dw_recv.at[slots_of[dest], cc], s_b, r_w.at[e], far[dest])

    dw_products(0)
    dw_products(1)
    dw_cores(0)
    dw_products(2)
    dw_cores(1)
    dw_cores(2)
    dw_x(0)
    dw_x(1)
    grad_rows(q_opp)
    recv(loss_v.at[q_p], r_l.at[1])
    recv(loss_v.at[q_opp], r_l.at[2])
    loss = (loss_v[0] + loss_v[1] + loss_v[2] + loss_v[3]) * (LN2 / (512 * 32))
    for q in range(4):
        loss_out[:, pl.ds(q * Q, Q)] = loss[q : q + 1]
    for e in range(3):
        cc = pl.ds(*CHUNKS[e])
        n_in = 7 if e < 2 else 15
        recv(dw_recv.at[pl.ds(0, n_in * 16), cc], r_w.at[e])
        total = dw_own[dest_rows(0, 0), cc]
        for n in range(n_in):
            total = total + dw_recv[pl.ds(n * 16, 16), cc].astype(F32)
        for row in range(14):
            dw_out[row, :, cc] = total[row : row + 1]
    for ss, n in ((s_a, 384 + 128 + 384), (s_z, 14 * 64 + 448), (s_x2, 1024), (s_sib, 2048), (s_b, 384 + 384 + 256 + 240)):
        sent(cols.at[pl.ds(0, n)], ss)
    sent(col_ids.at[0, pl.ds(0, 3)], s_i.at[0])
    sent(col_ids.at[pl.ds(0, 7)], s_i.at[1])
    sent(loss_v.at[pl.ds(0, 3)], s_l)


def hand_out(*refs):
    for n in range(3):
        refs[3 + n][...] = refs[n][...]


def local(inputs, weights, pair_ids):
    A = pltpu.VMEM
    dma = pltpu.SemaphoreType.DMA
    scratch = [
        A((512, E), BF16), A((Q, E), F32), A((Q, Q), F32), A((3, Q, E), F32),
        A((3, Q, E), BF16), A((4, 2, V, E), BF16), A((2, Q, E), BF16),
        A((4096, E), BF16), A((8, H, E), BF16), A((8, 4, 128), I32), A((512, 128), I32),
        A((512, 448), BF16), A((512, 512), BF16), A((256, 512), F32), A((256, 512), BF16),
        A((512, E), F32), A((512, 128), F32),
        A((3, Q, E), BF16), A((2, 2, W, E), BF16), A((2, Q, E), BF16),
        A((4, 4, 128), F32), A((512, E), BF16), A((256, E), F32), A((2, 256, E), BF16),
        A((256, E), BF16), A((240, E), BF16), A((128, E), BF16),
    ]
    for shape in (
        (), (), (), (), (), (2,), (),
        (4, 3, 2), (2, 3, 2), (10,), (3, 2), (2, 2), (2, 2, 2), (2, 3, 2), (2, 4, 2), (8, 2), (8,), (3,),
        (2,), (2, 3), (2, 3), (3,), (2,), (3,),
    ):
        scratch.append(dma(shape))
    vmem = pl.BlockSpec(memory_space=pltpu.VMEM)
    results = pl.pallas_call(
        kernel,
        out_shape=(
            jax.ShapeDtypeStruct((1, 512), F32),
            jax.ShapeDtypeStruct((448, 512), BF16),
            jax.ShapeDtypeStruct((14, 1, E), F32),
        ),
        in_specs=[vmem] * 3,
        out_specs=(vmem,) * 3,
        scratch_shapes=scratch,
        compiler_params=pltpu.CompilerParams(
            collective_id=0, has_side_effects=True, vmem_limit_bytes=56 * 2**20
        ),
        cost_estimate=pl.CostEstimate(flops=11 * 10**9, bytes_accessed=2 * 10**6, transcendentals=6 * 10**6),
    )(jnp.swapaxes(inputs[0], 0, 1), weights[0], pair_ids.reshape(4, 128))
    loss, dx, dw = pl.pallas_call(
        hand_out,
        out_shape=tuple(jax.ShapeDtypeStruct(a.shape, a.dtype) for a in results),
        in_specs=[vmem] * 3,
        out_specs=(vmem,) * 3,
    )(*results)
    return loss, jnp.swapaxes(dx, 0, 1)[None], dw.reshape(1, 14, E)


def solution(mesh):
    return jax.shard_map(
        local,
        mesh=mesh,
        in_specs=(P("tower", "dp", "mp"), P("tower", "mp", None), P("dp")),
        out_specs=(P("tower", "dp"), P("tower", "dp", "mp"), P("tower", ("mp", "dp"), None)),
        check_vma=False,
    )
```

```python
import jax
import jax.numpy as jnp
from jax import lax
from jax.experimental import pallas as pl
from jax.experimental.pallas import tpu as pltpu
from jax.sharding import PartitionSpec as P

MESH = pl.DeviceIdType.MESH
F32, BF16, I32 = jnp.float32, jnp.bfloat16, jnp.int32
LOGIT_SCALE = 100.0
LOGIT_BIAS = -6.0
NORM_EPS = 1e-06
LOG2E = 1.4426950408889634
LN2 = 0.6931471805599453

E = 1152
Q = 128
H = 64
W = 32
V = 16
CHUNKS = ((0, 384), (384, 384), (768, 384))
X_FIRST = (0, 1)
NT = (((1,), (1,)), ((), ()))
TN = (((0,), (0,)), ((), ()))


def kernel(xt_in, w_in, ids_in, loss_out, dx_out, dw_out, *scratch):
    (
        xt, w, ids, s_in,
        unit, unit_own, inv_own, part_f,
        e_send, e_opp, e_recv,
        cols, ring, col_ids, row_ids, sel, xpad, logits, slope, acc, lacc,
        g_send, g_opp, g_recv,
        loss_v, delta, dw_own, sib_dw, dw_send, dw_recv, dx_recv,
        s_a, s_z, s_x2, s_sib, s_b, s_i, s_l,
        r_e, r_g, r_i, r_u, r_x1, r_z0, r_z1, r_z2, r_x2, r_sib, r_l, r_d0, r_d1, r_df, r_ws, r_wx, r_w,
    ) = scratch
    t, d, m = lax.axis_index("tower"), lax.axis_index("dp"), lax.axis_index("mp")
    c, z, xh = lax.rem(d, 2), lax.rem(d // 2, 8), d // 16

    def at_dp(xh_, z_, c_):
        return (xh_ * 8 + z_) * 2 + c_

    def zoff(k):
        return lax.rem(z + (k + 8), 8)

    def moff(k):
        return lax.rem(m + (k + 4), 4)

    x_same, x_other = (1 - t, d, m), (1 - t, at_dp(1 - xh, z, c), m)
    y_dev = ((t, d, moff(1)), (t, d, moff(-1)))
    sibling = (t, at_dp(xh, z, 1 - c), m)
    far = {
        (dz, dx): (t, at_dp(1 - xh if dx else xh, zoff(dz), c), m)
        for dx in range(2) for dz in range(8) if dz or dx
    }
    z_dev = (far[1, 0], far[7, 0])
    x_far = far[0, 1]
    others = (x_same, x_other, *y_dev, sibling, *far.values())

    def send(src, dst, ss, rs, dev):
        pltpu.make_async_remote_copy(
            src_ref=src, dst_ref=dst, send_sem=ss, recv_sem=rs, device_id=dev, device_id_type=MESH
        ).start()

    def share(ref, ss, rs, dev):
        send(ref, ref, ss, rs, dev)

    def recv(dst, rs):
        pltpu.make_async_remote_copy(
            src_ref=dst, dst_ref=dst, send_sem=rs, recv_sem=rs, device_id=sibling, device_id_type=MESH
        ).wait_recv()

    def sent(ref, ss):
        pltpu.make_async_remote_copy(
            src_ref=ref, dst_ref=ref, send_sem=ss, recv_sem=ss, device_id=sibling, device_id_type=MESH
        ).wait_send()

    def rows_of(q, lo=0, n=Q):
        return pl.ds(pl.multiple_of(q * Q + lo, 16), n)

    q_opp, q_p, q_m = moff(2), moff(1), moff(-1)

    loads = [
        pltpu.make_async_copy(src, dst, s_in.at[n])
        for n, (src, dst) in enumerate(((xt_in, xt), (w_in, w), (ids_in, ids)))
    ]
    for load in loads:
        load.start()
    barrier = pltpu.get_barrier_semaphore()
    for dev in others:
        pl.semaphore_signal(barrier, inc=1, device_id=dev, device_id_type=MESH)

    def project(q):
        cc = pl.ds(pl.multiple_of(q * Q, Q), Q)
        return lax.dot_general(xt[:, cc], w[...], TN, preferred_element_type=F32)

    for load in loads:
        load.wait()
    e_send[0] = project(q_opp).astype(BF16)
    pl.semaphore_wait(barrier, len(others))

    def part(h, k, n):
        return pl.ds((2 * h + k) * n, n)

    def rs_opposite(h, buf, opp, ss, rs):
        n = opp.shape[2]
        for k in range(2):
            send(buf.at[0, part(h, k, n)], opp.at[h, k], ss, rs.at[h, 0, k], y_dev[k])

    def rs_direct(h, k, buf, got, ss, rs, n):
        p = part(h, 1 - k, n)
        send(buf.at[1 + k, p], got.at[k, p], ss, rs.at[h, 1, k], y_dev[k])

    def rs_sum(h, k, buf, opp, got, ss, rs, own):
        p = part(h, k, opp.shape[2])
        recv(opp.at[h, k], rs.at[h, 0, k])
        buf[1 + k, p, :] = (own + opp[h, k].astype(F32)).astype(BF16)
        send(buf.at[1 + k, p], got.at[k, p], ss, rs.at[h, 2, k], y_dev[k])

    def rs_total(h, got, rs, own, n):
        for k in range(2):
            recv(got.at[k, part(h, 1 - k, n)], rs.at[h, 1, k])
            recv(got.at[k, part(h, k, n)], rs.at[h, 2, k])
        rows = pl.ds(2 * h * n, 2 * n)
        return own + got[0, rows, :].astype(F32) + got[1, rows, :].astype(F32)

    def id_row(dc, dx):
        cc = 1 - c if dc else c
        xx = 1 - xh if dx else xh
        return col_ids.at[z, pl.ds(cc * 2 + xx, 1)]

    col_ids[z, pl.ds(c * 2 + xh, 1), :] = ids[pl.ds(m, 1), :]
    share(id_row(0, 0), s_i.at[0], r_i.at[0], x_far)
    share(id_row(0, 0), s_i.at[0], r_i.at[1], sibling)

    def ids_ring(s):
        share(col_ids.at[zoff(-s)], s_i.at[1], r_i.at[3 + 2 * s], z_dev[0])
        if s < 3:
            share(col_ids.at[zoff(s)], s_i.at[1], r_i.at[4 + 2 * s], z_dev[1])

    def ids_wait(s):
        recv(col_ids.at[zoff(-1 - s)], r_i.at[3 + 2 * s])
        if s < 3:
            recv(col_ids.at[zoff(1 + s)], r_i.at[4 + 2 * s])

    for h in range(4):
        rs_opposite(h, e_send, e_opp, s_a, r_e)
    for k, q in ((0, q_p), (1, q_m)):
        part_f[k] = project(q)
    for h in range(4):
        for k in range(2):
            p = part(h, 1 - k, V)
            e_send[1 + k, p, :] = part_f[k, p, :].astype(BF16)
            rs_direct(h, k, e_send, e_recv, s_a, r_e, V)
        for k in range(2):
            rs_sum(h, k, e_send, e_opp, e_recv, s_a, r_e, part_f[k, part(h, k, V), :])
    part_f[2] = project(m)
    recv(id_row(0, 1), r_i.at[0])
    recv(id_row(1, 0), r_i.at[1])
    share(id_row(0, 1), s_i.at[0], r_i.at[2], sibling)

    for q in range(4):
        row_ids[pl.ds(q * Q, Q), :] = jnp.transpose(jnp.broadcast_to(ids[pl.ds(q, 1), :], (Q, Q)))
    j = lax.broadcasted_iota(I32, (512, 448), 0)
    i = lax.broadcasted_iota(I32, (512, 448), 1)
    r = jnp.bitwise_and(j, 15)
    dest = (
        jnp.bitwise_and(jnp.right_shift(j, 7), 1) * 16
        + jnp.bitwise_and(jnp.right_shift(j, 4), 7) * 2
        + jnp.right_shift(j, 8)
    )
    sel[...] = jnp.where((i == dest * 14 + r) & (r < 14), 1.0, 0.0).astype(BF16)
    xpad[...] = jnp.dot(sel[...], xt[...], preferred_element_type=F32).astype(BF16)
    acc[...] = jnp.zeros_like(acc)
    lacc[...] = jnp.zeros_like(lacc)
    recv(id_row(1, 1), r_i.at[2])
    ids_ring(0)

    def normalise(h):
        rows = pl.ds(h * W, W)
        emb = rs_total(h, e_recv, r_e, part_f[2, rows, :], V)
        inv = lax.rsqrt(jnp.sum(emb * emb, axis=1, keepdims=True) + NORM_EPS)
        inv_own[rows, :] = jnp.broadcast_to(inv, (W, Q))
        uvec = emb * inv
        unit_own[rows, :] = uvec
        unit[rows_of(m, h * W, W), :] = uvec.astype(BF16)

    def block(z_, xh_, c_, lo, n):
        return cols.at[pl.ds(pl.multiple_of(((z_ * 2 + c_) * 2 + xh_) * Q + lo, 16), n)]

    def unit_rows(q, h):
        return unit.at[rows_of(q, h * H, H)]

    def ring_send(k, s, p, src):
        if s < 3 or p == k:
            zz = zoff(-s if k == 0 else s)
            send(src, ring.at[zz, pl.ds(p * W, W)], s_z, r_z2.at[k, s, p], z_dev[k])

    def ring_recv(k, s, p):
        zz = zoff(-s if k == 0 else s)
        piece = ring.at[zz, pl.ds(p * W, W)]
        if s < 4 or p == k:
            recv(piece, r_z2.at[k, s - 1, p])
        if s < 4:
            ring_send(k, s, p, piece)

    def across(zz, src):
        dst = block(zz, xh, c, 0, H)
        send(src, dst, s_x2, r_x2.at[zz, 0], x_same)
        send(src, dst, s_x2, r_x2.at[zz, 1], x_other)

    def across_recv(zz):
        for k in range(2):
            b = block(zz, xh if k == 0 else 1 - xh, c, 0, H)
            recv(b, r_x2.at[zz, k])
            share(b, s_sib, r_sib.at[zz], sibling)

    def to_sibling(zz, xk):
        share(block(zz, xk, c, H, H), s_sib, r_sib.at[zz], sibling)

    def z_first(p):
        for k in range(2):
            recv(block(z, xh if k == 0 else 1 - xh, c, H + p * W, W), r_x1.at[k, p])
        for i in range(2):
            for k in range(2):
                xk = (i + k) % 2
                share(block(z, xk, c, H + p * W, W), s_z, r_z0.at[k, xk, p], z_dev[k])

    def z_send(k, s, xk):
        share(block(zoff(-s if k == 0 else s), xk, c, H, H), s_z, r_z1.at[k, s - 1, xk], z_dev[k])

    def z_recv(k, s, xk):
        zz = zoff(-s if k == 0 else s)
        if s == 1:
            for p in range(2):
                recv(block(zz, xk, c, H + p * W, W), r_z0.at[k, xk, p])
        else:
            recv(block(zz, xk, c, H, H), r_z1.at[k, s - 2, xk])

    for h in range(4):
        normalise(h)
        own = unit.at[rows_of(m, h * W, W)]
        if h < 2:
            for k in range(2):
                ring_send(k, 0, h, own)
        else:
            dst = block(z, xh, c, h * W, W)
            send(own, dst, s_a, r_x1.at[0, h - 2], x_same)
            send(own, dst, s_a, r_x1.at[1, h - 2], x_other)
        if h % 2:
            for k in range(2):
                share(unit_rows(m, h // 2), s_a, r_u.at[h // 2, k], y_dev[k])
            ids_wait(h // 2)
            ids_ring(h // 2 + 1)
    across(z, unit_rows(m, 0))
    for p in range(2):
        for k in range(2):
            ring_recv(k, 1, p)
    for p in range(2):
        z_first(p)
    for xk in range(2):
        to_sibling(z, xk)

    def pair_logits(zz, rows):
        logits[rows, :] = lax.dot_general(
            unit[rows, :], cols[unit_cols(zz), :], NT, preferred_element_type=F32
        )

    def pair_terms(zz, rows):
        total = lacc[rows, :]
        rid = row_ids[rows, :]
        for jj in range(4):
            lc = pl.ds(jj * 128, 128)
            same = rid == col_ids[zz, pl.ds(jj, 1), :]
            lg = logits[rows, lc] * (LOGIT_SCALE * LOG2E) + (LOGIT_BIAS * LOG2E)
            v = jnp.where(same, -lg, lg)
            e = jnp.exp2(-jnp.abs(v))
            u = 1.0 + e
            lg1 = jnp.where(e < 2.0**-12, e * LOG2E, jnp.log2(u))
            total = total + (jnp.maximum(v, 0.0) + lg1)
            sg = jnp.where(v >= 0.0, 1.0, e) / u
            slope[rows, lc] = jnp.where(same, -sg, sg).astype(BF16)
        lacc[rows, :] = total

    def pair_grads(zz, rows):
        acc[rows, :] += jnp.dot(slope[rows, :], cols[unit_cols(zz), :], preferred_element_type=F32)

    def unit_cols(zz):
        return pl.ds(pl.multiple_of(zz * 512, 512), 512)

    def from_sibling(zz):
        rows = pl.ds(pl.multiple_of((zz * 2 + 1 - c) * 2 * Q, 2 * Q), 2 * Q)
        recv(cols.at[rows], r_sib.at[zz])

    def ring_step(s):
        for i in range(2):
            for k in range(2):
                ring_recv(k, s, (i + k) % 2)
        for k in range(1 if s == 4 else 2):
            across(zoff(s if k else -s), ring.at[zoff(s if k else -s)])

    def z_step(s, i):
        for k in range(2):
            xk = (i + k) % 2
            z_recv(k, s, xk)
            if s < 3 or (s == 3 and xk == k):
                z_send(k, s, xk)
        for k in range(2):
            to_sibling(zoff(s if k else -s), (i + k) % 2)

    def across_step(s):
        for k in range(1 if s == 4 else 2):
            across_recv(zoff(s if k else -s))

    ids_wait(2)
    ids_ring(3)
    for k in range(2):
        across(zoff(1 if k else -1), ring.at[zoff(1 if k else -1)])
    recv(unit_rows(q_m, 0), r_u.at[0, 0])
    share(unit_rows(q_m, 0), s_a, r_u.at[2, 0], y_dev[0])
    ring_step(2)
    across_recv(z)
    recv(unit_rows(q_p, 1), r_u.at[1, 1])
    share(unit_rows(q_p, 1), s_a, r_u.at[2, 1], y_dev[1])
    z_step(1, 0)
    z_step(1, 1)
    ids_wait(3)
    recv(unit_rows(q_p, 0), r_u.at[0, 1])
    recv(unit_rows(q_m, 1), r_u.at[1, 0])
    recv(unit_rows(q_opp, 0), r_u.at[2, 0])
    recv(unit_rows(q_opp, 1), r_u.at[2, 1])

    def pair_unit(u, carry):
        @pl.when(u == 1)
        def _():
            across_step(1)
            ring_step(3)

        @pl.when(u == 2)
        def _():
            z_step(2, 0)

        @pl.when(u == 3)
        def _():
            z_step(2, 1)
            across_step(2)

        @pl.when(u == 4)
        def _():
            ring_step(4)

        @pl.when(u == 5)
        def _():
            across_step(3)
            z_step(3, 0)
            z_step(3, 1)

        dist = (u + 1) // 2
        zz = lax.rem(z + jnp.where(lax.rem(u, 2) == 1, dist, 8 - dist), 8)
        from_sibling(zz)
        halves = pl.ds(0, 256), pl.ds(256, 256)
        pair_logits(zz, halves[0])
        pair_logits(zz, halves[1])
        pair_terms(zz, halves[0])
        pair_terms(zz, halves[1])
        pair_grads(zz, halves[0])
        pair_grads(zz, halves[1])
        return carry

    lax.fori_loop(0, 7, pair_unit, 0)
    z_step(4, 0)
    across_step(4)

    z_last = zoff(4)
    from_sibling(z_last)

    def last_quarter(n, carry):
        q = lax.rem(m + jnp.where(n == 0, 2, jnp.where(n == 1, 1, jnp.where(n == 2, 3, 0))), 4)
        rows = rows_of(q)
        pair_logits(z_last, rows)
        pair_terms(z_last, rows)
        pair_grads(z_last, rows)

        @pl.when(n < 3)
        def _():
            g_send[n] = acc[rows, :].astype(BF16)

        @pl.when(n == 0)
        def _():
            for h in range(2):
                rs_opposite(h, g_send, g_opp, s_b, r_g)

        @pl.when(n == 1)
        def _():
            rs_direct(0, 0, g_send, g_recv, s_b, r_g, W)

        @pl.when(n == 2)
        def _():
            rs_direct(0, 1, g_send, g_recv, s_b, r_g, W)

        return carry

    lax.fori_loop(0, 4, last_quarter, 0)
    for q in range(4):
        col = jnp.transpose(lacc[pl.ds(q * Q, Q), :])
        loss_v[m, pl.ds(q, 1), :] = jnp.sum(col, axis=0, keepdims=True)
    for h in range(2):
        if h:
            for k in range(2):
                rs_direct(1, k, g_send, g_recv, s_b, r_g, W)
        for k, q in ((0, q_p), (1, q_m)):
            rs_sum(h, k, g_send, g_opp, g_recv, s_b, r_g, acc[rows_of(q, h * H + k * W, W), :])
    for k in range(2):
        share(loss_v.at[m], s_l, r_l.at[k], y_dev[k])

    def back(h):
        rows = pl.ds(h * H, H)
        ug = rs_total(h, g_recv, r_g, acc[rows_of(m, h * H, H), :], W) * LOGIT_SCALE
        uvec = unit_own[rows, :]
        inner = jnp.sum(uvec * ug, axis=1, keepdims=True)
        delta[rows_of(m, h * H, H), :] = ((ug - uvec * inner) * inv_own[rows, 0:1]).astype(BF16)

    def delta_rows(q, h, e=None):
        rows = rows_of(q, h * H, H)
        return delta.at[rows] if e is None else delta.at[rows, pl.ds(*CHUNKS[e])]

    def grad_rows(q):
        dx_out[:, pl.ds(pl.multiple_of(q * Q, Q), Q)] = lax.dot_general(
            w[...], delta[rows_of(q), :], NT, preferred_element_type=F32
        ).astype(BF16)

    back(0)
    for k in range(2):
        share(delta_rows(m, 0), s_b, r_d0.at[k], y_dev[k])
    back(1)
    for e in range(len(CHUNKS)):
        for k in range(2):
            share(delta_rows(m, 1, e), s_b, r_d1.at[k, e], y_dev[k])
    grad_rows(m)
    recv(delta_rows(q_m, 0), r_d0.at[0])
    for e in range(len(CHUNKS)):
        share(delta_rows(q_m, 0, e), s_b, r_df.at[0, e], y_dev[0])
    recv(loss_v.at[q_m], r_l.at[0])
    share(loss_v.at[q_m], s_l, r_l.at[2], y_dev[0])
    for e in range(len(CHUNKS)):
        recv(delta_rows(q_p, 1, e), r_d1.at[1, e])
        share(delta_rows(q_p, 1, e), s_b, r_df.at[1, e], y_dev[1])
    recv(delta_rows(q_p, 0), r_d0.at[1])
    grad_rows(q_p)
    for e in range(len(CHUNKS)):
        recv(delta_rows(q_m, 1, e), r_d1.at[0, e])
    grad_rows(q_m)

    def dw_products(e):
        cc = pl.ds(*CHUNKS[e])
        recv(delta_rows(q_opp, 0, e), r_df.at[0, e])
        recv(delta_rows(q_opp, 1, e), r_df.at[1, e])
        for dc in range(2):
            rows = pl.ds(pl.multiple_of((c if dc else 1 - c) * 256, 256), 256)
            prod = jnp.dot(xpad[rows, :], delta[:, cc], preferred_element_type=F32)
            if dc:
                dw_own[:, cc] = prod
            else:
                sib_dw[0, :, cc] = prod.astype(BF16)
                send(sib_dw.at[0, :, cc], sib_dw.at[1, :, cc], s_b, r_ws.at[e], sibling)

    def x_rows(dx):
        return pl.ds(pl.multiple_of((1 - xh if dx else xh) * 128, 128), 128)

    def dest_rows(dz, dx):
        return pl.ds(pl.multiple_of(((1 - xh if dx else xh) * 8 + zoff(dz)) * 16, 16), 16)

    slots_of = {dest: pl.ds(n * 16, 16) for n, dest in enumerate(far)}

    def dw_cores(e):
        cc = pl.ds(*CHUNKS[e])
        recv(sib_dw.at[1, :, cc], r_ws.at[e])
        both = dw_own[:, cc] + sib_dw[1, :, cc].astype(F32)
        dw_own[:, cc] = both
        dw_send[:, cc] = both.astype(BF16)
        if e in X_FIRST:
            send(dw_send.at[x_rows(1), cc], dx_recv.at[:, cc], s_b, r_wx.at[e], x_far)
        else:
            dw_out_of(e, far)

    def dw_x(e):
        cc = pl.ds(*CHUNKS[e])
        recv(dx_recv.at[:, cc], r_wx.at[e])
        both = dw_own[x_rows(0), cc] + dx_recv[:, cc].astype(F32)
        dw_own[x_rows(0), cc] = both
        dw_send[x_rows(0), cc] = both.astype(BF16)
        dw_out_of(e, [dest for dest in far if not dest[1]])

    def dw_out_of(e, dests):
        cc = pl.ds(*CHUNKS[e])
        for dest in dests:
            send(dw_send.at[dest_rows(*dest), cc], dw_recv.at[slots_of[dest], cc], s_b, r_w.at[e], far[dest])

    n_chunks = len(CHUNKS)
    for e in range(n_chunks):
        dw_products(e)
        if e:
            dw_cores(e - 1)
    dw_cores(n_chunks - 1)
    for e in X_FIRST:
        dw_x(e)
    grad_rows(q_opp)
    recv(loss_v.at[q_p], r_l.at[1])
    recv(loss_v.at[q_opp], r_l.at[2])
    loss = (loss_v[0] + loss_v[1] + loss_v[2] + loss_v[3]) * (LN2 / (512 * 32))
    for q in range(4):
        loss_out[:, pl.ds(q * Q, Q)] = loss[q : q + 1]
    for e in range(len(CHUNKS)):
        cc = pl.ds(*CHUNKS[e])
        n_in = 7 if e in X_FIRST else 15
        recv(dw_recv.at[pl.ds(0, n_in * 16), cc], r_w.at[e])
        total = dw_own[dest_rows(0, 0), cc]
        for n in range(n_in):
            total = total + dw_recv[pl.ds(n * 16, 16), cc].astype(F32)
        for row in range(14):
            dw_out[row, :, cc] = total[row : row + 1]
    for ss, n in ((s_a, 384 + 128 + 384), (s_z, 14 * 64 + 448), (s_x2, 1024), (s_sib, 2048), (s_b, 384 + 384 + 256 + 240)):
        sent(cols.at[pl.ds(0, n)], ss)
    sent(col_ids.at[0, pl.ds(0, 3)], s_i.at[0])
    sent(col_ids.at[pl.ds(0, 7)], s_i.at[1])
    sent(loss_v.at[pl.ds(0, 3)], s_l)


def hand_out(*refs):
    for n in range(3):
        refs[3 + n][...] = refs[n][...]


def local(inputs, weights, pair_ids):
    A = pltpu.VMEM
    dma = pltpu.SemaphoreType.DMA
    scratch = [
        A((448, 512), BF16), A((448, E), BF16), A((4, 128), I32), dma((3,)),
        A((512, E), BF16), A((Q, E), F32), A((Q, Q), F32), A((3, Q, E), F32),
        A((3, Q, E), BF16), A((4, 2, V, E), BF16), A((2, Q, E), BF16),
        A((4096, E), BF16), A((8, H, E), BF16), A((8, 4, 128), I32), A((512, 128), I32),
        A((512, 448), BF16), A((512, 512), BF16), A((512, 512), F32), A((512, 512), BF16),
        A((512, E), F32), A((512, 128), F32),
        A((3, Q, E), BF16), A((2, 2, W, E), BF16), A((2, Q, E), BF16),
        A((4, 4, 128), F32), A((512, E), BF16), A((256, E), F32), A((2, 256, E), BF16),
        A((256, E), BF16), A((240, E), BF16), A((128, E), BF16),
    ]
    for shape in (
        (), (), (), (), (), (2,), (),
        (4, 3, 2), (2, 3, 2), (10,), (3, 2), (2, 2), (2, 2, 2), (2, 3, 2), (2, 4, 2), (8, 2), (8,), (3,),
        (2,), (2, 4), (2, 4), (4,), (4,), (4,),
    ):
        scratch.append(dma(shape))
    vmem = pl.BlockSpec(memory_space=pltpu.VMEM)
    results = pl.pallas_call(
        kernel,
        out_shape=(
            jax.ShapeDtypeStruct((1, 512), F32),
            jax.ShapeDtypeStruct((448, 512), BF16),
            jax.ShapeDtypeStruct((14, 1, E), F32),
        ),
        in_specs=[pl.BlockSpec(memory_space=pl.ANY)] * 3,
        out_specs=(vmem,) * 3,
        scratch_shapes=scratch,
        compiler_params=pltpu.CompilerParams(
            collective_id=0, has_side_effects=True, vmem_limit_bytes=56 * 2**20
        ),
        cost_estimate=pl.CostEstimate(flops=11 * 10**9, bytes_accessed=2 * 10**6, transcendentals=6 * 10**6),
    )(jnp.swapaxes(inputs[0], 0, 1), weights[0], pair_ids.reshape(4, 128))
    loss, dx, dw = pl.pallas_call(
        hand_out,
        out_shape=tuple(jax.ShapeDtypeStruct(a.shape, a.dtype) for a in results),
        in_specs=[vmem] * 3,
        out_specs=(vmem,) * 3,
    )(*results)
    return loss, jnp.swapaxes(dx, 0, 1)[None], dw.reshape(1, 14, E)


def solution(mesh):
    return jax.shard_map(
        local,
        mesh=mesh,
        in_specs=(P("tower", "dp", "mp"), P("tower", "mp", None), P("dp")),
        out_specs=(P("tower", "dp"), P("tower", "dp", "mp"), P("tower", ("mp", "dp"), None)),
        check_vma=False,
    )
```

```python
import jax
import jax.numpy as jnp
from jax import lax
from jax.experimental import pallas as pl
from jax.experimental.pallas import tpu as pltpu
from jax.sharding import PartitionSpec as P

MESH = pl.DeviceIdType.MESH
F32, BF16, I32 = jnp.float32, jnp.bfloat16, jnp.int32
LOGIT_SCALE = 100.0
LOGIT_BIAS = -6.0
NORM_EPS = 1e-06
LOG2E = 1.4426950408889634
LN2 = 0.6931471805599453

E = 1152
Q = 128
H = 64
W = 32
V = 16
CHUNKS = ((0, 384), (384, 384), (768, 384))
X_FIRST = (0, 1)
NT = (((1,), (1,)), ((), ()))
TN = (((0,), (0,)), ((), ()))


def kernel(xt_in, w_in, ids_in, loss_out, dx_out, dw_out, *scratch):
    (
        xt, w, ids, s_in,
        unit, unit_own, inv_own, part_f,
        e_send, e_opp, e_recv,
        cols, ring, col_ids, row_ids, sel, xpad, logits, slope, acc, lacc,
        g_send, g_opp, g_recv,
        loss_v, delta, dw_own, sib_dw, dw_send, dw_recv, dx_recv,
        s_a, s_z, s_x2, s_sib, s_b, s_i, s_l,
        r_e, r_g, r_i, r_u, r_x1, r_z0, r_z1, r_z2, r_x2, r_sib, r_l, r_d0, r_d1, r_df, r_ws, r_wx, r_w,
    ) = scratch
    t, d, m = lax.axis_index("tower"), lax.axis_index("dp"), lax.axis_index("mp")
    c, z, xh = lax.rem(d, 2), lax.rem(d // 2, 8), d // 16

    def at_dp(xh_, z_, c_):
        return (xh_ * 8 + z_) * 2 + c_

    def zoff(k):
        return lax.rem(z + (k + 8), 8)

    def moff(k):
        return lax.rem(m + (k + 4), 4)

    x_same, x_other = (1 - t, d, m), (1 - t, at_dp(1 - xh, z, c), m)
    y_dev = ((t, d, moff(1)), (t, d, moff(-1)))
    sibling = (t, at_dp(xh, z, 1 - c), m)
    far = {
        (dz, dx): (t, at_dp(1 - xh if dx else xh, zoff(dz), c), m)
        for dx in range(2) for dz in range(8) if dz or dx
    }
    z_dev = (far[1, 0], far[7, 0])
    x_far = far[0, 1]
    others = (x_same, x_other, *y_dev, sibling, *far.values())

    def send(src, dst, ss, rs, dev):
        pltpu.make_async_remote_copy(
            src_ref=src, dst_ref=dst, send_sem=ss, recv_sem=rs, device_id=dev, device_id_type=MESH
        ).start()

    def share(ref, ss, rs, dev):
        send(ref, ref, ss, rs, dev)

    def recv(dst, rs):
        pltpu.make_async_remote_copy(
            src_ref=dst, dst_ref=dst, send_sem=rs, recv_sem=rs, device_id=sibling, device_id_type=MESH
        ).wait_recv()

    def sent(ref, ss):
        pltpu.make_async_remote_copy(
            src_ref=ref, dst_ref=ref, send_sem=ss, recv_sem=ss, device_id=sibling, device_id_type=MESH
        ).wait_send()

    def rows_of(q, lo=0, n=Q):
        return pl.ds(pl.multiple_of(q * Q + lo, 16), n)

    q_opp, q_p, q_m = moff(2), moff(1), moff(-1)

    loads = [
        pltpu.make_async_copy(src, dst, s_in.at[n])
        for n, (src, dst) in enumerate(((xt_in, xt), (w_in, w), (ids_in, ids)))
    ]
    for load in loads:
        load.start()
    barrier = pltpu.get_barrier_semaphore()
    for dev in others:
        pl.semaphore_signal(barrier, inc=1, device_id=dev, device_id_type=MESH)

    def project(q):
        cc = pl.ds(pl.multiple_of(q * Q, Q), Q)
        return lax.dot_general(xt[:, cc], w[...], TN, preferred_element_type=F32)

    for load in loads:
        load.wait()
    e_send[0] = project(q_opp).astype(BF16)
    pl.semaphore_wait(barrier, len(others))

    def part(h, k, n):
        return pl.ds((2 * h + k) * n, n)

    def rs_opposite(h, buf, opp, ss, rs):
        n = opp.shape[2]
        for k in range(2):
            send(buf.at[0, part(h, k, n)], opp.at[h, k], ss, rs.at[h, 0, k], y_dev[k])

    def rs_direct(h, k, buf, got, ss, rs, n):
        p = part(h, 1 - k, n)
        send(buf.at[1 + k, p], got.at[k, p], ss, rs.at[h, 1, k], y_dev[k])

    def rs_sum(h, k, buf, opp, got, ss, rs, own):
        p = part(h, k, opp.shape[2])
        recv(opp.at[h, k], rs.at[h, 0, k])
        buf[1 + k, p, :] = (own + opp[h, k].astype(F32)).astype(BF16)
        send(buf.at[1 + k, p], got.at[k, p], ss, rs.at[h, 2, k], y_dev[k])

    def rs_total(h, got, rs, own, n):
        for k in range(2):
            recv(got.at[k, part(h, 1 - k, n)], rs.at[h, 1, k])
            recv(got.at[k, part(h, k, n)], rs.at[h, 2, k])
        rows = pl.ds(2 * h * n, 2 * n)
        return own + got[0, rows, :].astype(F32) + got[1, rows, :].astype(F32)

    def id_row(dc, dx):
        cc = 1 - c if dc else c
        xx = 1 - xh if dx else xh
        return col_ids.at[z, pl.ds(cc * 2 + xx, 1)]

    col_ids[z, pl.ds(c * 2 + xh, 1), :] = ids[pl.ds(m, 1), :]
    share(id_row(0, 0), s_i.at[0], r_i.at[0], x_far)
    share(id_row(0, 0), s_i.at[0], r_i.at[1], sibling)

    def ids_ring(s):
        share(col_ids.at[zoff(-s)], s_i.at[1], r_i.at[3 + 2 * s], z_dev[0])
        if s < 3:
            share(col_ids.at[zoff(s)], s_i.at[1], r_i.at[4 + 2 * s], z_dev[1])

    def ids_wait(s):
        recv(col_ids.at[zoff(-1 - s)], r_i.at[3 + 2 * s])
        if s < 3:
            recv(col_ids.at[zoff(1 + s)], r_i.at[4 + 2 * s])

    for h in range(4):
        rs_opposite(h, e_send, e_opp, s_a, r_e)
    for k, q in ((0, q_p), (1, q_m)):
        part_f[k] = project(q)
    for h in range(4):
        for k in range(2):
            p = part(h, 1 - k, V)
            e_send[1 + k, p, :] = part_f[k, p, :].astype(BF16)
            rs_direct(h, k, e_send, e_recv, s_a, r_e, V)
        for k in range(2):
            rs_sum(h, k, e_send, e_opp, e_recv, s_a, r_e, part_f[k, part(h, k, V), :])
    part_f[2] = project(m)
    recv(id_row(0, 1), r_i.at[0])
    recv(id_row(1, 0), r_i.at[1])
    share(id_row(0, 1), s_i.at[0], r_i.at[2], sibling)

    for q in range(4):
        row_ids[pl.ds(q * Q, Q), :] = jnp.transpose(jnp.broadcast_to(ids[pl.ds(q, 1), :], (Q, Q)))
    j = lax.broadcasted_iota(I32, (512, 448), 0)
    i = lax.broadcasted_iota(I32, (512, 448), 1)
    r = jnp.bitwise_and(j, 15)
    dest = (
        jnp.bitwise_and(jnp.right_shift(j, 7), 1) * 16
        + jnp.bitwise_and(jnp.right_shift(j, 4), 7) * 2
        + jnp.right_shift(j, 8)
    )
    sel[...] = jnp.where((i == dest * 14 + r) & (r < 14), 1.0, 0.0).astype(BF16)
    xpad[...] = jnp.dot(sel[...], xt[...], preferred_element_type=F32).astype(BF16)
    acc[...] = jnp.zeros_like(acc)
    lacc[...] = jnp.zeros_like(lacc)
    recv(id_row(1, 1), r_i.at[2])
    ids_ring(0)

    def normalise(h):
        rows = pl.ds(h * W, W)
        emb = rs_total(h, e_recv, r_e, part_f[2, rows, :], V)
        inv = lax.rsqrt(jnp.sum(emb * emb, axis=1, keepdims=True) + NORM_EPS)
        inv_own[rows, :] = jnp.broadcast_to(inv, (W, Q))
        uvec = emb * inv
        unit_own[rows, :] = uvec
        unit[rows_of(m, h * W, W), :] = uvec.astype(BF16)

    def block(z_, xh_, c_, lo, n):
        return cols.at[pl.ds(pl.multiple_of(((z_ * 2 + c_) * 2 + xh_) * Q + lo, 16), n)]

    def unit_rows(q, h):
        return unit.at[rows_of(q, h * H, H)]

    def ring_send(k, s, p, src):
        if s < 3 or p == k:
            zz = zoff(-s if k == 0 else s)
            send(src, ring.at[zz, pl.ds(p * W, W)], s_z, r_z2.at[k, s, p], z_dev[k])

    def ring_recv(k, s, p):
        zz = zoff(-s if k == 0 else s)
        piece = ring.at[zz, pl.ds(p * W, W)]
        if s < 4 or p == k:
            recv(piece, r_z2.at[k, s - 1, p])
        if s < 4:
            ring_send(k, s, p, piece)

    def across(zz, src):
        dst = block(zz, xh, c, 0, H)
        send(src, dst, s_x2, r_x2.at[zz, 0], x_same)
        send(src, dst, s_x2, r_x2.at[zz, 1], x_other)

    def across_recv(zz):
        for k in range(2):
            b = block(zz, xh if k == 0 else 1 - xh, c, 0, H)
            recv(b, r_x2.at[zz, k])
            share(b, s_sib, r_sib.at[zz], sibling)

    def to_sibling(zz, xk):
        share(block(zz, xk, c, H, H), s_sib, r_sib.at[zz], sibling)

    def z_first(p):
        for k in range(2):
            recv(block(z, xh if k == 0 else 1 - xh, c, H + p * W, W), r_x1.at[k, p])
        for i in range(2):
            for k in range(2):
                xk = (i + k) % 2
                share(block(z, xk, c, H + p * W, W), s_z, r_z0.at[k, xk, p], z_dev[k])

    def z_send(k, s, xk):
        share(block(zoff(-s if k == 0 else s), xk, c, H, H), s_z, r_z1.at[k, s - 1, xk], z_dev[k])

    def z_recv(k, s, xk):
        zz = zoff(-s if k == 0 else s)
        if s == 1:
            for p in range(2):
                recv(block(zz, xk, c, H + p * W, W), r_z0.at[k, xk, p])
        else:
            recv(block(zz, xk, c, H, H), r_z1.at[k, s - 2, xk])

    for h in range(4):
        normalise(h)
        own = unit.at[rows_of(m, h * W, W)]
        if h < 2:
            for k in range(2):
                ring_send(k, 0, h, own)
        else:
            dst = block(z, xh, c, h * W, W)
            send(own, dst, s_a, r_x1.at[0, h - 2], x_same)
            send(own, dst, s_a, r_x1.at[1, h - 2], x_other)
        if h % 2:
            for k in range(2):
                share(unit_rows(m, h // 2), s_a, r_u.at[h // 2, k], y_dev[k])
            ids_wait(h // 2)
            ids_ring(h // 2 + 1)
    across(z, unit_rows(m, 0))
    for p in range(2):
        for k in range(2):
            ring_recv(k, 1, p)
    for p in range(2):
        z_first(p)
    for xk in range(2):
        to_sibling(z, xk)

    def pair_logits(zz, rows):
        logits[rows, :] = lax.dot_general(
            unit[rows, :], cols[unit_cols(zz), :], NT, preferred_element_type=F32
        )

    def pair_terms(zz, rows):
        total = lacc[rows, :]
        rid = row_ids[rows, :]
        for jj in range(4):
            lc = pl.ds(jj * 128, 128)
            same = rid == col_ids[zz, pl.ds(jj, 1), :]
            lg = logits[rows, lc] * (LOGIT_SCALE * LOG2E) + (LOGIT_BIAS * LOG2E)
            v = jnp.where(same, -lg, lg)
            e = jnp.exp2(-jnp.abs(v))
            u = 1.0 + e
            lg1 = jnp.where(e < 2.0**-12, e * LOG2E, jnp.log2(u))
            total = total + (jnp.maximum(v, 0.0) + lg1)
            sg = jnp.where(v >= 0.0, 1.0, e) / u
            slope[rows, lc] = jnp.where(same, -sg, sg).astype(BF16)
        lacc[rows, :] = total

    def pair_grads(zz, rows):
        acc[rows, :] += jnp.dot(slope[rows, :], cols[unit_cols(zz), :], preferred_element_type=F32)

    def unit_cols(zz):
        return pl.ds(pl.multiple_of(zz * 512, 512), 512)

    def from_sibling(zz):
        rows = pl.ds(pl.multiple_of((zz * 2 + 1 - c) * 2 * Q, 2 * Q), 2 * Q)
        recv(cols.at[rows], r_sib.at[zz])

    def ring_step(s):
        for i in range(2):
            for k in range(2):
                ring_recv(k, s, (i + k) % 2)
        for k in range(1 if s == 4 else 2):
            across(zoff(s if k else -s), ring.at[zoff(s if k else -s)])

    def z_step(s, i):
        for k in range(2):
            xk = (i + k) % 2
            z_recv(k, s, xk)
            if s < 3 or (s == 3 and xk == k):
                z_send(k, s, xk)
        for k in range(2):
            to_sibling(zoff(s if k else -s), (i + k) % 2)

    def across_step(s):
        for k in range(1 if s == 4 else 2):
            across_recv(zoff(s if k else -s))

    ids_wait(2)
    ids_ring(3)
    for k in range(2):
        across(zoff(1 if k else -1), ring.at[zoff(1 if k else -1)])
    recv(unit_rows(q_m, 0), r_u.at[0, 0])
    share(unit_rows(q_m, 0), s_a, r_u.at[2, 0], y_dev[0])
    ring_step(2)
    across_recv(z)
    recv(unit_rows(q_p, 1), r_u.at[1, 1])
    share(unit_rows(q_p, 1), s_a, r_u.at[2, 1], y_dev[1])
    z_step(1, 0)
    z_step(1, 1)
    ids_wait(3)
    recv(unit_rows(q_p, 0), r_u.at[0, 1])
    recv(unit_rows(q_m, 1), r_u.at[1, 0])
    recv(unit_rows(q_opp, 0), r_u.at[2, 0])
    recv(unit_rows(q_opp, 1), r_u.at[2, 1])

    def pair_unit(u, carry):
        @pl.when(u == 1)
        def _():
            across_step(1)
            ring_step(3)

        @pl.when(u == 2)
        def _():
            z_step(2, 0)

        @pl.when(u == 3)
        def _():
            z_step(2, 1)
            across_step(2)

        @pl.when(u == 4)
        def _():
            ring_step(4)
            z_step(3, 0)

        @pl.when(u == 5)
        def _():
            across_step(3)
            z_step(3, 1)

        dist = (u + 1) // 2
        zz = lax.rem(z + jnp.where(lax.rem(u, 2) == 1, dist, 8 - dist), 8)
        from_sibling(zz)
        halves = pl.ds(0, 256), pl.ds(256, 256)
        pair_logits(zz, halves[0])
        pair_logits(zz, halves[1])
        pair_terms(zz, halves[0])
        pair_terms(zz, halves[1])
        pair_grads(zz, halves[0])
        pair_grads(zz, halves[1])
        return carry

    lax.fori_loop(0, 7, pair_unit, 0)
    z_step(4, 0)
    across_step(4)

    z_last = zoff(4)
    from_sibling(z_last)

    def last_quarter(n, carry):
        q = lax.rem(m + jnp.where(n == 0, 2, jnp.where(n == 1, 1, jnp.where(n == 2, 3, 0))), 4)
        rows = rows_of(q)
        pair_logits(z_last, rows)
        pair_terms(z_last, rows)
        pair_grads(z_last, rows)

        @pl.when(n < 3)
        def _():
            g_send[n] = acc[rows, :].astype(BF16)

        @pl.when(n == 0)
        def _():
            for h in range(2):
                rs_opposite(h, g_send, g_opp, s_b, r_g)

        @pl.when(n == 1)
        def _():
            rs_direct(0, 0, g_send, g_recv, s_b, r_g, W)

        @pl.when(n == 2)
        def _():
            rs_direct(0, 1, g_send, g_recv, s_b, r_g, W)

        return carry

    lax.fori_loop(0, 4, last_quarter, 0)
    for q in range(4):
        col = jnp.transpose(lacc[pl.ds(q * Q, Q), :])
        loss_v[m, pl.ds(q, 1), :] = jnp.sum(col, axis=0, keepdims=True)
    for h in range(2):
        if h:
            for k in range(2):
                rs_direct(1, k, g_send, g_recv, s_b, r_g, W)
        for k, q in ((0, q_p), (1, q_m)):
            rs_sum(h, k, g_send, g_opp, g_recv, s_b, r_g, acc[rows_of(q, h * H + k * W, W), :])
    for k in range(2):
        share(loss_v.at[m], s_l, r_l.at[k], y_dev[k])

    def back(h):
        rows = pl.ds(h * H, H)
        ug = rs_total(h, g_recv, r_g, acc[rows_of(m, h * H, H), :], W) * LOGIT_SCALE
        uvec = unit_own[rows, :]
        inner = jnp.sum(uvec * ug, axis=1, keepdims=True)
        delta[rows_of(m, h * H, H), :] = ((ug - uvec * inner) * inv_own[rows, 0:1]).astype(BF16)

    def delta_rows(q, h, e=None):
        rows = rows_of(q, h * H, H)
        return delta.at[rows] if e is None else delta.at[rows, pl.ds(*CHUNKS[e])]

    def grad_rows(q):
        dx_out[:, pl.ds(pl.multiple_of(q * Q, Q), Q)] = lax.dot_general(
            w[...], delta[rows_of(q), :], NT, preferred_element_type=F32
        ).astype(BF16)

    back(0)
    for k in range(2):
        share(delta_rows(m, 0), s_b, r_d0.at[k], y_dev[k])
    back(1)
    for e in range(len(CHUNKS)):
        for k in range(2):
            share(delta_rows(m, 1, e), s_b, r_d1.at[k, e], y_dev[k])
    grad_rows(m)
    recv(delta_rows(q_m, 0), r_d0.at[0])
    for e in range(len(CHUNKS)):
        share(delta_rows(q_m, 0, e), s_b, r_df.at[0, e], y_dev[0])
    recv(loss_v.at[q_m], r_l.at[0])
    share(loss_v.at[q_m], s_l, r_l.at[2], y_dev[0])
    for e in range(len(CHUNKS)):
        recv(delta_rows(q_p, 1, e), r_d1.at[1, e])
        share(delta_rows(q_p, 1, e), s_b, r_df.at[1, e], y_dev[1])
    recv(delta_rows(q_p, 0), r_d0.at[1])
    grad_rows(q_p)
    for e in range(len(CHUNKS)):
        recv(delta_rows(q_m, 1, e), r_d1.at[0, e])
    grad_rows(q_m)

    def dw_products(e):
        cc = pl.ds(*CHUNKS[e])
        recv(delta_rows(q_opp, 0, e), r_df.at[0, e])
        recv(delta_rows(q_opp, 1, e), r_df.at[1, e])
        for dc in range(2):
            rows = pl.ds(pl.multiple_of((c if dc else 1 - c) * 256, 256), 256)
            prod = jnp.dot(xpad[rows, :], delta[:, cc], preferred_element_type=F32)
            if dc:
                dw_own[:, cc] = prod
            else:
                sib_dw[0, :, cc] = prod.astype(BF16)
                send(sib_dw.at[0, :, cc], sib_dw.at[1, :, cc], s_b, r_ws.at[e], sibling)

    def x_rows(dx):
        return pl.ds(pl.multiple_of((1 - xh if dx else xh) * 128, 128), 128)

    def dest_rows(dz, dx):
        return pl.ds(pl.multiple_of(((1 - xh if dx else xh) * 8 + zoff(dz)) * 16, 16), 16)

    slots_of = {dest: pl.ds(n * 16, 16) for n, dest in enumerate(far)}

    def dw_cores(e):
        cc = pl.ds(*CHUNKS[e])
        recv(sib_dw.at[1, :, cc], r_ws.at[e])
        both = dw_own[:, cc] + sib_dw[1, :, cc].astype(F32)
        dw_own[:, cc] = both
        dw_send[:, cc] = both.astype(BF16)
        if e in X_FIRST:
            send(dw_send.at[x_rows(1), cc], dx_recv.at[:, cc], s_b, r_wx.at[e], x_far)
        else:
            dw_out_of(e, far)

    def dw_x(e):
        cc = pl.ds(*CHUNKS[e])
        recv(dx_recv.at[:, cc], r_wx.at[e])
        both = dw_own[x_rows(0), cc] + dx_recv[:, cc].astype(F32)
        dw_own[x_rows(0), cc] = both
        dw_send[x_rows(0), cc] = both.astype(BF16)
        dw_out_of(e, [dest for dest in far if not dest[1]])

    def dw_out_of(e, dests):
        cc = pl.ds(*CHUNKS[e])
        for dest in dests:
            send(dw_send.at[dest_rows(*dest), cc], dw_recv.at[slots_of[dest], cc], s_b, r_w.at[e], far[dest])

    n_chunks = len(CHUNKS)
    for e in range(n_chunks):
        dw_products(e)
        if e:
            dw_cores(e - 1)
    dw_cores(n_chunks - 1)
    for e in X_FIRST:
        dw_x(e)
    grad_rows(q_opp)
    recv(loss_v.at[q_p], r_l.at[1])
    recv(loss_v.at[q_opp], r_l.at[2])
    loss = (loss_v[0] + loss_v[1] + loss_v[2] + loss_v[3]) * (LN2 / (512 * 32))
    for q in range(4):
        loss_out[:, pl.ds(q * Q, Q)] = loss[q : q + 1]
    for e in range(len(CHUNKS)):
        cc = pl.ds(*CHUNKS[e])
        n_in = 7 if e in X_FIRST else 15
        recv(dw_recv.at[pl.ds(0, n_in * 16), cc], r_w.at[e])
        total = dw_own[dest_rows(0, 0), cc]
        for n in range(n_in):
            total = total + dw_recv[pl.ds(n * 16, 16), cc].astype(F32)
        for row in range(14):
            dw_out[row, :, cc] = total[row : row + 1]
    for ss, n in ((s_a, 384 + 128 + 384), (s_z, 14 * 64 + 448), (s_x2, 1024), (s_sib, 2048), (s_b, 384 + 384 + 256 + 240)):
        sent(cols.at[pl.ds(0, n)], ss)
    sent(col_ids.at[0, pl.ds(0, 3)], s_i.at[0])
    sent(col_ids.at[pl.ds(0, 7)], s_i.at[1])
    sent(loss_v.at[pl.ds(0, 3)], s_l)


def local(inputs, weights, pair_ids):
    A = pltpu.VMEM
    dma = pltpu.SemaphoreType.DMA
    scratch = [
        A((448, 512), BF16), A((448, E), BF16), A((4, 128), I32), dma((3,)),
        A((512, E), BF16), A((Q, E), F32), A((Q, Q), F32), A((3, Q, E), F32),
        A((3, Q, E), BF16), A((4, 2, V, E), BF16), A((2, Q, E), BF16),
        A((4096, E), BF16), A((8, H, E), BF16), A((8, 4, 128), I32), A((512, 128), I32),
        A((512, 448), BF16), A((512, 512), BF16), A((512, 512), F32), A((512, 512), BF16),
        A((512, E), F32), A((512, 128), F32),
        A((3, Q, E), BF16), A((2, 2, W, E), BF16), A((2, Q, E), BF16),
        A((4, 4, 128), F32), A((512, E), BF16), A((256, E), F32), A((2, 256, E), BF16),
        A((256, E), BF16), A((240, E), BF16), A((128, E), BF16),
    ]
    for shape in (
        (), (), (), (), (), (2,), (),
        (4, 3, 2), (2, 3, 2), (10,), (3, 2), (2, 2), (2, 2, 2), (2, 3, 2), (2, 4, 2), (8, 2), (8,), (3,),
        (2,), (2, 4), (2, 4), (4,), (4,), (4,),
    ):
        scratch.append(dma(shape))
    vmem = pl.BlockSpec(memory_space=pltpu.VMEM)
    loss, dx, dw = pl.pallas_call(
        kernel,
        out_shape=(
            pltpu.VMEM((1, 512), F32),
            pltpu.VMEM((448, 512), BF16),
            pltpu.VMEM((14, 1, E), F32),
        ),
        in_specs=[pl.BlockSpec(memory_space=pl.ANY)] * 3,
        out_specs=(vmem,) * 3,
        scratch_shapes=scratch,
        compiler_params=pltpu.CompilerParams(
            collective_id=0, has_side_effects=True, vmem_limit_bytes=56 * 2**20
        ),
        cost_estimate=pl.CostEstimate(flops=11 * 10**9, bytes_accessed=2 * 10**6, transcendentals=6 * 10**6),
    )(jnp.swapaxes(inputs[0], 0, 1), weights[0], pair_ids.reshape(4, 128))
    return loss, jnp.swapaxes(dx, 0, 1)[None], dw.reshape(1, 14, E)


def solution(mesh):
    return jax.shard_map(
        local,
        mesh=mesh,
        in_specs=(P("tower", "dp", "mp"), P("tower", "mp", None), P("dp")),
        out_specs=(P("tower", "dp"), P("tower", "dp", "mp"), P("tower", ("mp", "dp"), None)),
        check_vma=False,
    )
```

```python
import jax
import jax.numpy as jnp
from jax import lax
from jax.experimental import pallas as pl
from jax.experimental.pallas import tpu as pltpu
from jax.sharding import PartitionSpec as P

MESH = pl.DeviceIdType.MESH
F32, BF16, I32 = jnp.float32, jnp.bfloat16, jnp.int32
LOGIT_SCALE = 100.0
LOGIT_BIAS = -6.0
NORM_EPS = 1e-06
LOG2E = 1.4426950408889634
LN2 = 0.6931471805599453

E = 1152
Q = 128
H = 64
W = 32
V = 16
CHUNKS = ((0, 384), (384, 384), (768, 384))
X_FIRST = (0, 1)
NT = (((1,), (1,)), ((), ()))
TN = (((0,), (0,)), ((), ()))


def kernel(xt_in, w_in, ids_in, loss_out, dx_out, dw_out, *scratch):
    (
        xt, w, ids, s_in,
        unit, unit_own, inv_own, part_f,
        e_send, e_opp, e_recv,
        cols, ring, col_ids, row_ids, sel, xpad, logits, slope, acc, lacc,
        g_send, g_opp, g_recv,
        loss_v, delta, dw_own, sib_dw, dw_send, dw_recv, dx_recv,
        s_a, s_z, s_x2, s_sib, s_b, s_i, s_l,
        r_e, r_g, r_i, r_u, r_x1, r_z0, r_z1, r_z2, r_x2, r_sib, r_l, r_d0, r_d1, r_df, r_ws, r_wx, r_w,
    ) = scratch
    t, d, m = lax.axis_index("tower"), lax.axis_index("dp"), lax.axis_index("mp")
    c, z, xh = lax.rem(d, 2), lax.rem(d // 2, 8), d // 16

    def at_dp(xh_, z_, c_):
        return (xh_ * 8 + z_) * 2 + c_

    def zoff(k):
        return lax.rem(z + (k + 8), 8)

    def moff(k):
        return lax.rem(m + (k + 4), 4)

    x_same, x_other = (1 - t, d, m), (1 - t, at_dp(1 - xh, z, c), m)
    y_dev = ((t, d, moff(1)), (t, d, moff(-1)))
    sibling = (t, at_dp(xh, z, 1 - c), m)
    far = {
        (dz, dx): (t, at_dp(1 - xh if dx else xh, zoff(dz), c), m)
        for dx in range(2) for dz in range(8) if dz or dx
    }
    z_dev = (far[1, 0], far[7, 0])
    x_far = far[0, 1]
    others = (x_same, x_other, *y_dev, sibling, *z_dev, x_far)

    def send(src, dst, ss, rs, dev):
        pltpu.make_async_remote_copy(
            src_ref=src, dst_ref=dst, send_sem=ss, recv_sem=rs, device_id=dev, device_id_type=MESH
        ).start()

    def share(ref, ss, rs, dev):
        send(ref, ref, ss, rs, dev)

    def recv(dst, rs):
        pltpu.make_async_remote_copy(
            src_ref=dst, dst_ref=dst, send_sem=rs, recv_sem=rs, device_id=sibling, device_id_type=MESH
        ).wait_recv()

    def sent(ref, ss):
        pltpu.make_async_remote_copy(
            src_ref=ref, dst_ref=ref, send_sem=ss, recv_sem=ss, device_id=sibling, device_id_type=MESH
        ).wait_send()

    def rows_of(q, lo=0, n=Q):
        return pl.ds(pl.multiple_of(q * Q + lo, 16), n)

    q_opp, q_p, q_m = moff(2), moff(1), moff(-1)

    loads = [
        pltpu.make_async_copy(src, dst, s_in.at[n])
        for n, (src, dst) in enumerate(((xt_in, xt), (w_in, w), (ids_in, ids)))
    ]
    for load in loads:
        load.start()
    barrier = pltpu.get_barrier_semaphore()
    for dev in others:
        pl.semaphore_signal(barrier, inc=1, device_id=dev, device_id_type=MESH)

    def project(q):
        cc = pl.ds(pl.multiple_of(q * Q, Q), Q)
        return lax.dot_general(xt[:, cc], w[...], TN, preferred_element_type=F32)

    for load in loads:
        load.wait()
    e_send[0] = project(q_opp).astype(BF16)
    pl.semaphore_wait(barrier, len(others))

    def part(h, k, n):
        return pl.ds((2 * h + k) * n, n)

    def rs_opposite(h, buf, opp, ss, rs):
        n = opp.shape[2]
        for k in range(2):
            send(buf.at[0, part(h, k, n)], opp.at[h, k], ss, rs.at[h, 0, k], y_dev[k])

    def rs_direct(h, k, buf, got, ss, rs, n):
        p = part(h, 1 - k, n)
        send(buf.at[1 + k, p], got.at[k, p], ss, rs.at[h, 1, k], y_dev[k])

    def rs_sum(h, k, buf, opp, got, ss, rs, own):
        p = part(h, k, opp.shape[2])
        recv(opp.at[h, k], rs.at[h, 0, k])
        buf[1 + k, p, :] = (own + opp[h, k].astype(F32)).astype(BF16)
        send(buf.at[1 + k, p], got.at[k, p], ss, rs.at[h, 2, k], y_dev[k])

    def rs_total(h, got, rs, own, n):
        for k in range(2):
            recv(got.at[k, part(h, 1 - k, n)], rs.at[h, 1, k])
            recv(got.at[k, part(h, k, n)], rs.at[h, 2, k])
        rows = pl.ds(2 * h * n, 2 * n)
        return own + got[0, rows, :].astype(F32) + got[1, rows, :].astype(F32)

    def id_row(dc, dx):
        cc = 1 - c if dc else c
        xx = 1 - xh if dx else xh
        return col_ids.at[z, pl.ds(cc * 2 + xx, 1)]

    col_ids[z, pl.ds(c * 2 + xh, 1), :] = ids[pl.ds(m, 1), :]
    share(id_row(0, 0), s_i.at[0], r_i.at[0], x_far)
    share(id_row(0, 0), s_i.at[0], r_i.at[1], sibling)

    def ids_ring(s):
        share(col_ids.at[zoff(-s)], s_i.at[1], r_i.at[3 + 2 * s], z_dev[0])
        if s < 3:
            share(col_ids.at[zoff(s)], s_i.at[1], r_i.at[4 + 2 * s], z_dev[1])

    def ids_wait(s):
        recv(col_ids.at[zoff(-1 - s)], r_i.at[3 + 2 * s])
        if s < 3:
            recv(col_ids.at[zoff(1 + s)], r_i.at[4 + 2 * s])

    for h in range(4):
        rs_opposite(h, e_send, e_opp, s_a, r_e)
    for k, q in ((0, q_p), (1, q_m)):
        part_f[k] = project(q)
    for h in range(4):
        for k in range(2):
            p = part(h, 1 - k, V)
            e_send[1 + k, p, :] = part_f[k, p, :].astype(BF16)
            rs_direct(h, k, e_send, e_recv, s_a, r_e, V)
        for k in range(2):
            rs_sum(h, k, e_send, e_opp, e_recv, s_a, r_e, part_f[k, part(h, k, V), :])
    part_f[2] = project(m)
    recv(id_row(0, 1), r_i.at[0])
    recv(id_row(1, 0), r_i.at[1])
    share(id_row(0, 1), s_i.at[0], r_i.at[2], sibling)

    for q in range(4):
        row_ids[pl.ds(q * Q, Q), :] = jnp.transpose(jnp.broadcast_to(ids[pl.ds(q, 1), :], (Q, Q)))
    j = lax.broadcasted_iota(I32, (512, 448), 0)
    i = lax.broadcasted_iota(I32, (512, 448), 1)
    r = jnp.bitwise_and(j, 15)
    dest = (
        jnp.bitwise_and(jnp.right_shift(j, 7), 1) * 16
        + jnp.bitwise_and(jnp.right_shift(j, 4), 7) * 2
        + jnp.right_shift(j, 8)
    )
    sel[...] = jnp.where((i == dest * 14 + r) & (r < 14), 1.0, 0.0).astype(BF16)
    xpad[...] = jnp.dot(sel[...], xt[...], preferred_element_type=F32).astype(BF16)
    acc[...] = jnp.zeros_like(acc)
    lacc[...] = jnp.zeros_like(lacc)
    recv(id_row(1, 1), r_i.at[2])
    ids_ring(0)

    def normalise(h):
        rows = pl.ds(h * W, W)
        emb = rs_total(h, e_recv, r_e, part_f[2, rows, :], V)
        inv = lax.rsqrt(jnp.sum(emb * emb, axis=1, keepdims=True) + NORM_EPS)
        inv_own[rows, :] = jnp.broadcast_to(inv, (W, Q))
        uvec = emb * inv
        unit_own[rows, :] = uvec
        unit[rows_of(m, h * W, W), :] = uvec.astype(BF16)

    def block(z_, xh_, c_, lo, n):
        return cols.at[pl.ds(pl.multiple_of(((z_ * 2 + c_) * 2 + xh_) * Q + lo, 16), n)]

    def unit_rows(q, h):
        return unit.at[rows_of(q, h * H, H)]

    def ring_send(k, s, p, src):
        if s < 3 or p == k:
            zz = zoff(-s if k == 0 else s)
            send(src, ring.at[zz, pl.ds(p * W, W)], s_z, r_z2.at[k, s, p], z_dev[k])

    def ring_recv(k, s, p):
        zz = zoff(-s if k == 0 else s)
        piece = ring.at[zz, pl.ds(p * W, W)]
        if s < 4 or p == k:
            recv(piece, r_z2.at[k, s - 1, p])
        if s < 4:
            ring_send(k, s, p, piece)

    def across(zz, src):
        dst = block(zz, xh, c, 0, H)
        send(src, dst, s_x2, r_x2.at[zz, 0], x_same)
        send(src, dst, s_x2, r_x2.at[zz, 1], x_other)

    def across_recv(zz):
        for k in range(2):
            b = block(zz, xh if k == 0 else 1 - xh, c, 0, H)
            recv(b, r_x2.at[zz, k])
            share(b, s_sib, r_sib.at[zz], sibling)

    def to_sibling(zz, xk):
        share(block(zz, xk, c, H, H), s_sib, r_sib.at[zz], sibling)

    def z_first(p):
        for k in range(2):
            recv(block(z, xh if k == 0 else 1 - xh, c, H + p * W, W), r_x1.at[k, p])
        for i in range(2):
            for k in range(2):
                xk = (i + k) % 2
                share(block(z, xk, c, H + p * W, W), s_z, r_z0.at[k, xk, p], z_dev[k])

    def z_send(k, s, xk):
        share(block(zoff(-s if k == 0 else s), xk, c, H, H), s_z, r_z1.at[k, s - 1, xk], z_dev[k])

    def z_recv(k, s, xk):
        zz = zoff(-s if k == 0 else s)
        if s == 1:
            for p in range(2):
                recv(block(zz, xk, c, H + p * W, W), r_z0.at[k, xk, p])
        else:
            recv(block(zz, xk, c, H, H), r_z1.at[k, s - 2, xk])

    for h in range(4):
        normalise(h)
        own = unit.at[rows_of(m, h * W, W)]
        if h < 2:
            for k in range(2):
                ring_send(k, 0, h, own)
        else:
            dst = block(z, xh, c, h * W, W)
            send(own, dst, s_a, r_x1.at[0, h - 2], x_same)
            send(own, dst, s_a, r_x1.at[1, h - 2], x_other)
        if h % 2:
            for k in range(2):
                share(unit_rows(m, h // 2), s_a, r_u.at[h // 2, k], y_dev[k])
            ids_wait(h // 2)
            ids_ring(h // 2 + 1)
    across(z, unit_rows(m, 0))
    for p in range(2):
        for k in range(2):
            ring_recv(k, 1, p)
    for p in range(2):
        z_first(p)
    for xk in range(2):
        to_sibling(z, xk)

    def pair_logits(zz, rows):
        logits[rows, :] = lax.dot_general(
            unit[rows, :], cols[unit_cols(zz), :], NT, preferred_element_type=F32
        )

    def pair_terms(zz, rows):
        total = lacc[rows, :]
        rid = row_ids[rows, :]
        for jj in range(4):
            lc = pl.ds(jj * 128, 128)
            same = rid == col_ids[zz, pl.ds(jj, 1), :]
            lg = logits[rows, lc] * (LOGIT_SCALE * LOG2E) + (LOGIT_BIAS * LOG2E)
            v = jnp.where(same, -lg, lg)
            e = jnp.exp2(-jnp.abs(v))
            u = 1.0 + e
            lg1 = jnp.where(e < 2.0**-12, e * LOG2E, jnp.log2(u))
            total = total + (jnp.maximum(v, 0.0) + lg1)
            sg = jnp.where(v >= 0.0, 1.0, e) / u
            slope[rows, lc] = jnp.where(same, -sg, sg).astype(BF16)
        lacc[rows, :] = total

    def pair_grads(zz, rows):
        acc[rows, :] += jnp.dot(slope[rows, :], cols[unit_cols(zz), :], preferred_element_type=F32)

    def unit_cols(zz):
        return pl.ds(pl.multiple_of(zz * 512, 512), 512)

    def from_sibling(zz):
        rows = pl.ds(pl.multiple_of((zz * 2 + 1 - c) * 2 * Q, 2 * Q), 2 * Q)
        recv(cols.at[rows], r_sib.at[zz])

    def ring_step(s):
        for i in range(2):
            for k in range(2):
                ring_recv(k, s, (i + k) % 2)
        for k in range(1 if s == 4 else 2):
            across(zoff(s if k else -s), ring.at[zoff(s if k else -s)])

    def z_step(s, i):
        for k in range(2):
            xk = (i + k) % 2
            z_recv(k, s, xk)
            if s < 3 or (s == 3 and xk == k):
                z_send(k, s, xk)
        for k in range(2):
            to_sibling(zoff(s if k else -s), (i + k) % 2)

    def across_step(s):
        for k in range(1 if s == 4 else 2):
            across_recv(zoff(s if k else -s))

    ids_wait(2)
    ids_ring(3)
    for k in range(2):
        across(zoff(1 if k else -1), ring.at[zoff(1 if k else -1)])
    recv(unit_rows(q_m, 0), r_u.at[0, 0])
    share(unit_rows(q_m, 0), s_a, r_u.at[2, 0], y_dev[0])
    ring_step(2)
    across_recv(z)
    recv(unit_rows(q_p, 1), r_u.at[1, 1])
    share(unit_rows(q_p, 1), s_a, r_u.at[2, 1], y_dev[1])
    z_step(1, 0)
    z_step(1, 1)
    ids_wait(3)
    recv(unit_rows(q_p, 0), r_u.at[0, 1])
    recv(unit_rows(q_m, 1), r_u.at[1, 0])
    recv(unit_rows(q_opp, 0), r_u.at[2, 0])
    recv(unit_rows(q_opp, 1), r_u.at[2, 1])

    def pair_unit(u, carry):
        @pl.when(u == 1)
        def _():
            across_step(1)
            ring_step(3)

        @pl.when(u == 2)
        def _():
            z_step(2, 0)

        @pl.when(u == 3)
        def _():
            z_step(2, 1)
            across_step(2)

        @pl.when(u == 4)
        def _():
            ring_step(4)
            z_step(3, 0)

        @pl.when(u == 5)
        def _():
            across_step(3)
            z_step(3, 1)

        dist = (u + 1) // 2
        zz = lax.rem(z + jnp.where(lax.rem(u, 2) == 1, dist, 8 - dist), 8)
        from_sibling(zz)
        halves = pl.ds(0, 256), pl.ds(256, 256)
        pair_logits(zz, halves[0])
        pair_logits(zz, halves[1])
        pair_terms(zz, halves[0])
        pair_terms(zz, halves[1])
        pair_grads(zz, halves[0])
        pair_grads(zz, halves[1])
        return carry

    lax.fori_loop(0, 7, pair_unit, 0)
    z_step(4, 0)
    across_step(4)

    z_last = zoff(4)
    from_sibling(z_last)

    def last_quarter(n, carry):
        q = lax.rem(m + jnp.where(n == 0, 2, jnp.where(n == 1, 1, jnp.where(n == 2, 3, 0))), 4)
        rows = rows_of(q)
        pair_logits(z_last, rows)
        pair_terms(z_last, rows)
        pair_grads(z_last, rows)

        @pl.when(n < 3)
        def _():
            g_send[n] = acc[rows, :].astype(BF16)

        @pl.when(n == 0)
        def _():
            for h in range(2):
                rs_opposite(h, g_send, g_opp, s_b, r_g)

        @pl.when(n == 1)
        def _():
            rs_direct(0, 0, g_send, g_recv, s_b, r_g, W)

        @pl.when(n == 2)
        def _():
            rs_direct(0, 1, g_send, g_recv, s_b, r_g, W)

        return carry

    lax.fori_loop(0, 4, last_quarter, 0)
    for q in range(4):
        col = jnp.transpose(lacc[pl.ds(q * Q, Q), :])
        loss_v[m, pl.ds(q, 1), :] = jnp.sum(col, axis=0, keepdims=True)
    for h in range(2):
        if h:
            for k in range(2):
                rs_direct(1, k, g_send, g_recv, s_b, r_g, W)
        for k, q in ((0, q_p), (1, q_m)):
            rs_sum(h, k, g_send, g_opp, g_recv, s_b, r_g, acc[rows_of(q, h * H + k * W, W), :])
    for k in range(2):
        share(loss_v.at[m], s_l, r_l.at[k], y_dev[k])

    def back(h):
        rows = pl.ds(h * H, H)
        ug = rs_total(h, g_recv, r_g, acc[rows_of(m, h * H, H), :], W) * LOGIT_SCALE
        uvec = unit_own[rows, :]
        inner = jnp.sum(uvec * ug, axis=1, keepdims=True)
        delta[rows_of(m, h * H, H), :] = ((ug - uvec * inner) * inv_own[rows, 0:1]).astype(BF16)

    def delta_rows(q, h, e=None):
        rows = rows_of(q, h * H, H)
        return delta.at[rows] if e is None else delta.at[rows, pl.ds(*CHUNKS[e])]

    def grad_rows(q):
        dx_out[:, pl.ds(pl.multiple_of(q * Q, Q), Q)] = lax.dot_general(
            w[...], delta[rows_of(q), :], NT, preferred_element_type=F32
        ).astype(BF16)

    back(0)
    for k in range(2):
        share(delta_rows(m, 0), s_b, r_d0.at[k], y_dev[k])
    back(1)
    for e in range(len(CHUNKS)):
        for k in range(2):
            share(delta_rows(m, 1, e), s_b, r_d1.at[k, e], y_dev[k])
    grad_rows(m)
    recv(delta_rows(q_m, 0), r_d0.at[0])
    for e in range(len(CHUNKS)):
        share(delta_rows(q_m, 0, e), s_b, r_df.at[0, e], y_dev[0])
    recv(loss_v.at[q_m], r_l.at[0])
    share(loss_v.at[q_m], s_l, r_l.at[2], y_dev[0])
    for e in range(len(CHUNKS)):
        recv(delta_rows(q_p, 1, e), r_d1.at[1, e])
        share(delta_rows(q_p, 1, e), s_b, r_df.at[1, e], y_dev[1])
    recv(delta_rows(q_p, 0), r_d0.at[1])
    grad_rows(q_p)
    for e in range(len(CHUNKS)):
        recv(delta_rows(q_m, 1, e), r_d1.at[0, e])
    grad_rows(q_m)

    def dw_products(e):
        cc = pl.ds(*CHUNKS[e])
        recv(delta_rows(q_opp, 0, e), r_df.at[0, e])
        recv(delta_rows(q_opp, 1, e), r_df.at[1, e])
        for dc in range(2):
            rows = pl.ds(pl.multiple_of((c if dc else 1 - c) * 256, 256), 256)
            prod = jnp.dot(xpad[rows, :], delta[:, cc], preferred_element_type=F32)
            if dc:
                dw_own[:, cc] = prod
            else:
                sib_dw[0, :, cc] = prod.astype(BF16)
                send(sib_dw.at[0, :, cc], sib_dw.at[1, :, cc], s_b, r_ws.at[e], sibling)

    def x_rows(dx):
        return pl.ds(pl.multiple_of((1 - xh if dx else xh) * 128, 128), 128)

    def dest_rows(dz, dx):
        return pl.ds(pl.multiple_of(((1 - xh if dx else xh) * 8 + zoff(dz)) * 16, 16), 16)

    slots_of = {dest: pl.ds(n * 16, 16) for n, dest in enumerate(far)}

    def dw_cores(e):
        cc = pl.ds(*CHUNKS[e])
        recv(sib_dw.at[1, :, cc], r_ws.at[e])
        both = dw_own[:, cc] + sib_dw[1, :, cc].astype(F32)
        dw_own[:, cc] = both
        dw_send[:, cc] = both.astype(BF16)
        if e in X_FIRST:
            send(dw_send.at[x_rows(1), cc], dx_recv.at[:, cc], s_b, r_wx.at[e], x_far)
        else:
            dw_out_of(e, far)

    def dw_x(e):
        cc = pl.ds(*CHUNKS[e])
        recv(dx_recv.at[:, cc], r_wx.at[e])
        both = dw_own[x_rows(0), cc] + dx_recv[:, cc].astype(F32)
        dw_own[x_rows(0), cc] = both
        dw_send[x_rows(0), cc] = both.astype(BF16)
        dw_out_of(e, [dest for dest in far if not dest[1]])

    def dw_out_of(e, dests):
        cc = pl.ds(*CHUNKS[e])
        for dest in dests:
            send(dw_send.at[dest_rows(*dest), cc], dw_recv.at[slots_of[dest], cc], s_b, r_w.at[e], far[dest])

    n_chunks = len(CHUNKS)
    for e in range(n_chunks):
        dw_products(e)
        if e:
            dw_cores(e - 1)
    dw_cores(n_chunks - 1)
    for e in X_FIRST:
        dw_x(e)
    grad_rows(q_opp)
    recv(loss_v.at[q_p], r_l.at[1])
    recv(loss_v.at[q_opp], r_l.at[2])
    loss = (loss_v[0] + loss_v[1] + loss_v[2] + loss_v[3]) * (LN2 / (512 * 32))
    for q in range(4):
        loss_out[:, pl.ds(q * Q, Q)] = loss[q : q + 1]
    for e in range(len(CHUNKS)):
        cc = pl.ds(*CHUNKS[e])
        n_in = 7 if e in X_FIRST else 15
        recv(dw_recv.at[pl.ds(0, n_in * 16), cc], r_w.at[e])
        total = dw_own[dest_rows(0, 0), cc]
        for n in range(n_in):
            total = total + dw_recv[pl.ds(n * 16, 16), cc].astype(F32)
        for row in range(14):
            dw_out[row, :, cc] = total[row : row + 1]
    for ss, n in ((s_a, 384 + 128 + 384), (s_z, 14 * 64 + 448), (s_x2, 1024), (s_sib, 2048), (s_b, 384 + 384 + 256 + 240)):
        sent(cols.at[pl.ds(0, n)], ss)
    sent(col_ids.at[0, pl.ds(0, 3)], s_i.at[0])
    sent(col_ids.at[pl.ds(0, 7)], s_i.at[1])
    sent(loss_v.at[pl.ds(0, 3)], s_l)


def local(inputs, weights, pair_ids):
    A = pltpu.VMEM
    dma = pltpu.SemaphoreType.DMA
    scratch = [
        A((448, 512), BF16), A((448, E), BF16), A((4, 128), I32), dma((3,)),
        A((512, E), BF16), A((Q, E), F32), A((Q, Q), F32), A((3, Q, E), F32),
        A((3, Q, E), BF16), A((4, 2, V, E), BF16), A((2, Q, E), BF16),
        A((4096, E), BF16), A((8, H, E), BF16), A((8, 4, 128), I32), A((512, 128), I32),
        A((512, 448), BF16), A((512, 512), BF16), A((512, 512), F32), A((512, 512), BF16),
        A((512, E), F32), A((512, 128), F32),
        A((3, Q, E), BF16), A((2, 2, W, E), BF16), A((2, Q, E), BF16),
        A((4, 4, 128), F32), A((512, E), BF16), A((256, E), F32), A((2, 256, E), BF16),
        A((256, E), BF16), A((240, E), BF16), A((128, E), BF16),
    ]
    for shape in (
        (), (), (), (), (), (2,), (),
        (4, 3, 2), (2, 3, 2), (10,), (3, 2), (2, 2), (2, 2, 2), (2, 3, 2), (2, 4, 2), (8, 2), (8,), (3,),
        (2,), (2, 4), (2, 4), (4,), (4,), (4,),
    ):
        scratch.append(dma(shape))
    vmem = pl.BlockSpec(memory_space=pltpu.VMEM)
    loss, dx, dw = pl.pallas_call(
        kernel,
        out_shape=(
            pltpu.VMEM((1, 512), F32),
            pltpu.VMEM((448, 512), BF16),
            pltpu.VMEM((14, 1, E), F32),
        ),
        in_specs=[pl.BlockSpec(memory_space=pl.ANY)] * 3,
        out_specs=(vmem,) * 3,
        scratch_shapes=scratch,
        compiler_params=pltpu.CompilerParams(
            collective_id=0, has_side_effects=True, vmem_limit_bytes=56 * 2**20
        ),
        cost_estimate=pl.CostEstimate(flops=11 * 10**9, bytes_accessed=2 * 10**6, transcendentals=6 * 10**6),
    )(jnp.swapaxes(inputs[0], 0, 1), weights[0], pair_ids.reshape(4, 128))
    return loss, jnp.swapaxes(dx, 0, 1)[None], dw.reshape(1, 14, E)


def solution(mesh):
    return jax.shard_map(
        local,
        mesh=mesh,
        in_specs=(P("tower", "dp", "mp"), P("tower", "mp", None), P("dp")),
        out_specs=(P("tower", "dp"), P("tower", "dp", "mp"), P("tower", ("mp", "dp"), None)),
        check_vma=False,
    )
```
